256 devices in a mesh: dp: 8 (over x, core), seq: 32 (over z, y).
Axes of the slice: x: 4, y: 4, z: 8, core: 2. Of those that a mesh axis runs over, the one named last changes fastest.
Arguments:
- activations: bfloat16 [4, 16384, 6144], P(None, ('dp', 'seq')), may hold values from -16 to 16
- prev_basis: bfloat16 [4, 1536, 512], replicated, may hold values from -0.15625 to 0.15625
Outputs:
- new_basis: float32 [6144, 512], P('seq')
The draws below stay inside these ranges and needn't reach their ends.
All inputs are finite; a program needn't handle non-finite values.
Results may differ from the reference program's by a relative error of at most 0.0085.
Values may be sent and summed in bfloat16 or wider, within the bound.
A program may use at most 128 MiB of HBM per device.

```python
import math
import jax
import jax.numpy as jnp
from jax import lax

D = 6144
BLOCK = 1536
K = 512
MICRO = 4
TOKENS = 16384
NBLK = 4


def draw_activations(key, part):
    key = jax.random.fold_in(key, 11)
    col_key, row_key, value_key = jax.random.split(key, 3)
    col_scale = jnp.exp(jax.random.uniform(col_key, (D,), jnp.float32, math.log(0.5), math.log(2.0)))
    row_scale = jnp.exp(jax.random.uniform(row_key, (MICRO, TOKENS, 1), jnp.float32, math.log(0.5), math.log(2.0)))
    sample = jnp.clip(jax.random.normal(value_key, (MICRO, TOKENS, D), jnp.float32), -4.0, 4.0)
    return (sample * row_scale * col_scale).astype(jnp.bfloat16)


def bell_draw(rng, extent, spread, most, kind=jnp.bfloat16):
    return jnp.clip(spread * jax.random.normal(rng, extent, jnp.float32), -most, most).astype(kind)


def setup_inputs(seed: int = 0) -> dict:
    key_list = jax.random.split(jax.random.key(seed), 3)
    activations = draw_activations(jax.random.fold_in(key_list[2], 71), 0)
    prev_basis = bell_draw(key_list[1], (NBLK, BLOCK, K), BLOCK ** -0.5, 0.15625)
    return {"activations": activations, "prev_basis": prev_basis}


def reference(activations, prev_basis):
    flat_rows = activations.reshape(MICRO * TOKENS, D)
    token_total = MICRO * TOKENS

    def one_block(block_idx):
        columns = lax.dynamic_slice_in_dim(flat_rows, block_idx * BLOCK, BLOCK, 1)
        block_basis = lax.dynamic_index_in_dim(prev_basis, block_idx, 0, keepdims=False)
        projected = jnp.dot(columns.astype(jnp.float32), block_basis.astype(jnp.float32), preferred_element_type=jnp.float32).astype(jnp.bfloat16)
        panel = jnp.dot(columns.T.astype(jnp.float32), projected.astype(jnp.float32), preferred_element_type=jnp.float32) / token_total
        gram_small = jnp.dot(panel.T, panel, precision=lax.Precision.HIGHEST)
        factor = jnp.linalg.cholesky(gram_small)
        solved = jax.scipy.linalg.solve_triangular(factor, panel.T, lower=True)
        return solved.T * math.sqrt(BLOCK)
    result = lax.map(one_block, jnp.arange(D // BLOCK, dtype=jnp.int32))
    return result.reshape(D, K)
```

```python
import math

import jax
import jax.numpy as jnp
from jax import lax
from jax.experimental import pallas as pl
from jax.experimental.pallas import tpu as pltpu
from jax.sharding import PartitionSpec as P

HI = lax.Precision.HIGHEST

def diag_inverse(groups):
    n = len(groups)
    a = list(groups)
    sub = lax.broadcasted_iota(jnp.int32, (8, 128), 0)
    lane = lax.broadcasted_iota(jnp.int32, (8, 128), 1)
    out = []
    for s in range(n):
        c0 = 8 * s
        r = a[s]
        b = [jnp.broadcast_to(r[:, c0 + j:c0 + j + 1], (8, 128)) for j in range(8)]
        pivinv = jnp.zeros((8, 128), jnp.float32)
        for k in range(8):
            p = jnp.broadcast_to(b[k][k:k + 1, :], (8, 128))
            inv = 1.0 / p
            m = jnp.where(sub > k, b[k] * inv, 0.0)
            pivinv = jnp.where(sub == k, inv, pivinv)
            if k < 7:
                rowk = jnp.broadcast_to(r[k:k + 1, :], (8, 128))
                rowk = jnp.where(lane == c0 + k, 1.0, rowk)
                rz = jnp.where((lane == c0 + k) & (sub > k), 0.0, r)
                r = rz - m * rowk
                for j in range(k + 1, 8):
                    b[j] = b[j] - m * jnp.broadcast_to(b[j][k:k + 1, :], (8, 128))
        rel = lane - c0 - sub
        rp = jnp.where(rel == 0, 1.0, jnp.where((rel > 0) & (lane < c0 + 8), 0.0, r))
        if s + 1 < n:
            un = r * pivinv
            ut = un.T
            for t in range(s + 1, n):
                tt = ut[8 * t:8 * t + 8, :]
                acc = jnp.where((lane >= c0) & (lane < c0 + 8), 0.0, a[t])
                for k in range(8):
                    acc = acc - jnp.broadcast_to(tt[:, k:k + 1], (8, 128)) * jnp.broadcast_to(rp[k:k + 1, :], (8, 128))
                a[t] = acc
        out.append(jnp.where(lane < c0 + 8, rp, 0.0) * jnp.sqrt(pivinv))
    return out

def chol_kernel(g_ref, p_ref, o_ref, a_ref):
    K = g_ref.shape[0]
    R = p_ref.shape[0]
    nb = K // 128
    a_ref[0:K, :] = g_ref[...]
    a_ref[K:K + R, :] = p_ref[...]
    scale = math.sqrt(1536.0)
    for b in range(nb):
        lo = 128 * b
        tiles = [a_ref[lo + 8 * i:lo + 8 * i + 8, lo:lo + 128] for i in range(16)]
        x = jnp.concatenate(diag_inverse(tiles), axis=0)
        m = lax.dot_general(a_ref[lo + 128:, lo:lo + 128], x, (((1,), (1,)), ((), ())), precision=HI, preferred_element_type=jnp.float32)
        nrest = K - lo - 128
        o_ref[:, lo:lo + 128] = m[nrest:, :] * scale
        for c in range(b + 1, nb):
            off = 128 * (c - b - 1)
            a_ref[128 * c:, 128 * c:128 * c + 128] -= lax.dot_general(m[off:, :], m[off:off + 128, :], (((1,), (1,)), ((), ())), precision=HI, preferred_element_type=jnp.float32)

def chol_solve(g, p):
    return pl.pallas_call(chol_kernel, out_shape=jax.ShapeDtypeStruct(p.shape, jnp.float32),
        in_specs=[pl.BlockSpec(memory_space=pltpu.VMEM)] * 2, out_specs=pl.BlockSpec(memory_space=pltpu.VMEM),
        scratch_shapes=[pltpu.VMEM((g.shape[0] + p.shape[0], g.shape[0]), jnp.float32)],
        compiler_params=pltpu.CompilerParams(vmem_limit_bytes=32 * 2**20))(g, p)


def swapped(value, axis, bit):
    mask = 2**bit
    pairs = [(source, source ^ mask) for source in range(lax.axis_size(axis))]
    return lax.ppermute(value, axis, pairs)


def contract_rows(left_side, right_side):
    return lax.dot_general(
        left_side, right_side, (((0,), (0,)), ((), ())), preferred_element_type=jnp.float32
    )


def on_device(activations, prev_basis):
    blocks = prev_basis.shape[0]
    block_width = prev_basis.shape[1]
    basis_cols = prev_basis.shape[2]
    micro_count = activations.shape[0]
    seq_count = lax.axis_size("seq")
    groups = seq_count // blocks
    group_bits = groups.bit_length() - 1
    position = lax.axis_index("seq")
    member = position % groups
    token_total = micro_count * activations.shape[1] * lax.axis_size("dp") * seq_count
    block_basis = lax.dynamic_index_in_dim(prev_basis, position // groups, 0, keepdims=False)
    partial_sum = jnp.zeros((block_width, basis_cols), jnp.float32)
    for micro_idx in range(micro_count):
        token_rows = activations[micro_idx]
        per_group = token_rows.shape[0] // groups
        outgoing = token_rows.reshape(groups, per_group, blocks, block_width)
        outgoing = outgoing.transpose(2, 0, 1, 3).reshape(seq_count, per_group, block_width)
        arrived = lax.all_to_all(outgoing, "seq", split_axis=0, concat_axis=1, tiled=True).reshape(
            -1, block_width
        )
        projected = jnp.dot(arrived, block_basis, preferred_element_type=jnp.float32).astype(
            jnp.bfloat16
        )
        partial_sum = partial_sum + contract_rows(arrived, projected)
    partial_sum = lax.psum(partial_sum, "dp")
    for bit_pos in reversed(range(group_bits)):
        half_rows = partial_sum.shape[0] // 2
        upper_half = member // (1 << bit_pos) % 2
        kept_half = lax.dynamic_slice_in_dim(partial_sum, upper_half * half_rows, half_rows, 0)
        handed = lax.dynamic_slice_in_dim(partial_sum, (1 - upper_half) * half_rows, half_rows, 0)
        partial_sum = kept_half + swapped(handed, "seq", bit_pos)
    panel = partial_sum / token_total
    gram_small = jnp.dot(panel.T, panel, precision=lax.Precision.HIGHEST)
    for bit_pos in range(group_bits):
        gram_small = gram_small + swapped(gram_small, "seq", bit_pos)
    return chol_solve(gram_small, panel)


def solution(mesh):
    in_specs = (P(None, ("dp", "seq"), None), P())
    out_specs = P("seq", None)
    return jax.shard_map(
        on_device, mesh=mesh, in_specs=in_specs, out_specs=out_specs, check_vma=False
    )
```

```python
import math

import jax
import jax.numpy as jnp
from jax import lax
from jax.experimental import pallas as pl
from jax.experimental.pallas import tpu as pltpu
from jax.sharding import PartitionSpec as P

F32, BF16 = jnp.float32, jnp.bfloat16
NX, NC, NZ, NY = 4, 2, 8, 4
HI = lax.Precision.HIGHEST
STAGES = (("z", "y", "x"), ("y", "x", "z"), ("x", "z", "y"))
SIZE = {"x": NX, "y": NY, "z": NZ}


class Copies:
    def __init__(self, send_sems, recv_sems):
        self.send_sems, self.recv_sems, self.count, self.made = send_sems, recv_sems, 0, []

    def send(self, src, dst, device):
        n = self.count
        self.count += 1
        copy = pltpu.make_async_remote_copy(
            src_ref=src, dst_ref=dst, send_sem=self.send_sems.at[n], recv_sem=self.recv_sems.at[n],
            device_id=device, device_id_type=pl.DeviceIdType.MESH,
        )
        copy.start()
        self.made.append(copy)
        return copy


def ring(copies, n, me, piece, half, to, up_s, up_r, dn_s, dn_r, up_h, dn_h, up_hr, dn_hr):
    steps = n // 2
    far = piece(lax.rem(me + steps, n))
    up_h[...] = far[:half].astype(BF16)
    dn_h[...] = far[half:].astype(BF16)
    up = copies.send(up_h, up_hr, to(lax.rem(me + 1, n)))
    dn = copies.send(dn_h, dn_hr, to(lax.rem(me + n - 1, n)))
    yield
    for i in range(1, steps):
        d = steps - i
        mine = piece(lax.rem(me + d, n))
        up.wait_recv()
        if i == 1:
            up_s[0, :half] = (mine[:half] + up_hr[...].astype(F32)).astype(BF16)
            up_s[0, half:] = mine[half:].astype(BF16)
        else:
            up_s[i - 1] = (mine + up_r[i - 2].astype(F32)).astype(BF16)
        up = copies.send(up_s.at[i - 1], up_r.at[i - 1], to(lax.rem(me + 1, n)))
        mine = piece(lax.rem(me + n - d, n))
        dn.wait_recv()
        if i == 1:
            dn_s[0, half:] = (mine[half:] + dn_hr[...].astype(F32)).astype(BF16)
            dn_s[0, :half] = mine[:half].astype(BF16)
        else:
            dn_s[i - 1] = (mine + dn_r[i - 2].astype(F32)).astype(BF16)
        dn = copies.send(dn_s.at[i - 1], dn_r.at[i - 1], to(lax.rem(me + n - 1, n)))
        yield
    up.wait_recv()
    dn.wait_recv()
    return piece(me) + up_r[steps - 2].astype(F32) + dn_r[steps - 2].astype(F32)


def direct(copies, n, me, piece, to, bufs, bufr):
    sent = []
    for d in range(1, n):
        bufs[d - 1] = piece(lax.rem(me + d, n)).astype(bufs.dtype)
        sent.append(copies.send(bufs.at[d - 1], bufr.at[d - 1], to(lax.rem(me + d, n))))
    yield
    total = piece(me)
    for d in range(1, n):
        sent[d - 1].wait_recv()
        total = total + bufr[d - 1].astype(F32)
    return total


def kernel(act, basis, p_out, g_out, *scratch):
    (a_v, b_v, proj, pan, p_v, g_v, gs, gsum, gr, load_sems, send_sems, recv_sems, out_sems,
     *bufs) = scratch
    bufs = list(bufs)
    dp, seq = lax.axis_index("dp"), lax.axis_index("seq")
    x, c, z, y = dp // 2, lax.rem(dp, 2), seq // NY, lax.rem(seq, NY)
    zz = lax.rem(z, 2)
    me = {"x": x, "y": y, "z": z}

    def dev(x_=None, c_=None, z_=None, y_=None):
        x_, c_, z_, y_ = (x if x_ is None else x_, c if c_ is None else c_,
                          z if z_ is None else z_, y if y_ is None else y_)
        return (x_ * NC + c_, z_ * NY + y_)

    order = [lax.rem(z // 2 + o, 4) for o in (2, 1, 3, 0)]
    own_loads, b_loads = [], []
    for i, j in enumerate(order):
        cols = pl.ds(pl.multiple_of(j * 1536, 1536), 1536)
        b_loads.append(pltpu.make_async_copy(
            basis.at[j, :, pl.ds(pl.multiple_of(c * 256, 256), 256)], b_v.at[i], load_sems.at[i]))
        own_loads.append(pltpu.make_async_copy(act.at[:, :, cols], a_v.at[i, 0], load_sems.at[4 + i]))
        own_loads[i].start()
        b_loads[i].start()

    peers = [dev(c_=1 - c)]
    for d in range(1, NX):
        peers += [dev(x_=lax.rem(x + d, NX)), dev(x_=lax.rem(x + d, NX), c_=1 - c)]
    for d in range(1, NY):
        peers += [dev(y_=lax.rem(y + d, NY)), dev(z_=z + 1 - 2 * zz, y_=lax.rem(y + d, NY))]
    for d in range(1, NZ):
        peers.append(dev(z_=lax.rem(z + d, NZ)))
    barrier = pltpu.get_barrier_semaphore()
    for peer in peers:
        pl.semaphore_signal(barrier, inc=1, device_id=peer, device_id_type=pl.DeviceIdType.MESH)
    pl.semaphore_wait(barrier, len(peers))

    copies = Copies(send_sems, recv_sems)
    exchanged = []
    for i, j in enumerate(order):
        cols = pl.ds(pl.multiple_of(j * 1536, 1536), 1536)
        exchanged.append(copies.send(act.at[:, :, cols], a_v.at[i, 1], dev(c_=1 - c)))

    shares = [8 + 1 + 2 + 1 + 2] * 3
    pools = []
    for share in shares:
        pools.append(bufs[:share])
        bufs = bufs[share:]

    def stream_with(t, pool):
        axes = STAGES[t]
        pool = list(pool)
        cur = pan.at[t]
        left = ["z", "y", "x"]
        for stage, axis in enumerate(axes):
            n = SIZE[axis]
            pos = left.index(axis)
            left.pop(pos)

            def piece(dest, cur=cur, pos=pos):
                return cur[(slice(None),) * pos + (dest,)]

            def to(dest, axis=axis):
                return dev(**{axis + "_": dest})

            if stage == 0:
                taken, pool = pool[:8], pool[8:]
                total = yield from ring(copies, n, me[axis], piece, taken[4].shape[0], to, *taken)
            else:
                taken, pool = pool[:2], pool[2:]
                total = yield from direct(copies, n, me[axis], piece, to, *taken)
            if stage < 2:
                cur = pool.pop(0)
                cur[...] = total
            else:
                p_v[c, x, 16 * t:16 * t + 16, :] = total * (1.0 / 65536.0)

    gens = [stream_with(t, pools[t]) for t in range(3)]

    def compute(i):
        j = order[i]
        b_loads[i].wait()
        own_loads[i].wait()
        proj[0:256, :] = jnp.dot(a_v[i, 0].reshape(256, 1536), b_v[i], preferred_element_type=F32).astype(BF16)
        exchanged[i].wait_recv()
        proj[256:512, :] = jnp.dot(a_v[i, 1].reshape(256, 1536), b_v[i], preferred_element_type=F32).astype(BF16)
        for k in range(4):
            lhs = a_v[i, :, :, :, 384 * k:384 * k + 384].reshape(512, 384)
            r = lax.dot_general(lhs, proj[...], (((0,), (0,)), ((), ())), preferred_element_type=F32)
            r = r.reshape(2, 4, 3, 16, 256)
            for t in range(3):
                pan[t, 2 * j + k // 2, 2 * (k % 2):2 * (k % 2) + 2] = r[:, :, t]

    compute(0)
    next(gens[0])
    for i in range(1, 4):
        compute(i)
    live = [1, 2, 0]
    while live:
        for t in list(live):
            try:
                next(gens[t])
            except StopIteration:
                live.remove(t)

    sent = []
    for d in range(1, 8):
        sent.append(copies.send(p_v.at[c, x], p_v.at[c, x],
                                dev(x_=lax.rem(x + d // 2, NX), c_=c if d % 2 == 0 else 1 - c)))
    for copy in sent:
        copy.wait_recv()

    blk = p_v[x // 2, :, :, pl.ds(pl.multiple_of(lax.rem(x, 2) * 128, 128), 128)].reshape(192, 128)
    for h in range(2):
        gs[:, :, 256 * h:256 * h + 256] = lax.dot_general(
            blk, p_v[h].reshape(192, 256), (((0,), (0,)), ((), ())), precision=HI,
            preferred_element_type=F32).reshape(16, 8, 256)
    p_me = zz * NY + y
    sent = []
    for d in range(1, 8):
        q = lax.rem(p_me + d, 8)
        sent.append(copies.send(gs.at[8 * c + q], gr.at[d - 1], dev(z_=z - zz + q // NY, y_=lax.rem(q, NY))))
    total = gs[8 * c + p_me]
    for d in range(1, 8):
        sent[d - 1].wait_recv()
        total = total + gr[d - 1]
    g_v[c, x, p_me] = total
    sent = []
    for d in range(1, 8):
        q = lax.rem(p_me + d, 8)
        sent.append(copies.send(g_v.at[c, x, p_me], g_v.at[c, x, p_me], dev(z_=z - zz + q // NY, y_=lax.rem(q, NY))))
    for copy in sent:
        copy.wait_recv()
    sent = []
    for d in range(1, NX):
        sent.append(copies.send(g_v.at[c, x], g_v.at[c, x], dev(x_=lax.rem(x + d, NX))))
    for copy in sent:
        copy.wait_recv()
    last = copies.send(g_v.at[c], g_v.at[c], dev(c_=1 - c))
    p_done = pltpu.make_async_copy(p_v, p_out, out_sems.at[0])
    p_done.start()
    last.wait_recv()
    g_done = pltpu.make_async_copy(g_v, g_out, out_sems.at[1])
    g_done.start()
    for copy in copies.made:
        copy.wait_send()
    p_done.wait()
    g_done.wait()


def panel_and_gram(act, basis):
    piece = {"x": (NZ, NY), "y": (NZ, NX), "z": (NY, NX)}
    tile = (16, 256)
    bufs = []
    for axes in STAGES:
        left = ["z", "y", "x"]
        for stage, axis in enumerate(axes):
            left.remove(axis)
            n = SIZE[axis]
            shape = tuple(SIZE[a] for a in left) + tile
            if stage == 0:
                half = (shape[0] // 2,) + shape[1:]
                full = (n // 2 - 1,) + shape
                bufs += [pltpu.VMEM(full, BF16)] * 4 + [pltpu.VMEM(half, BF16)] * 4
            else:
                bufs += [pltpu.VMEM((n - 1,) + shape, BF16 if stage == 1 else F32)] * 2
            if stage < 2:
                bufs.append(pltpu.VMEM(shape, F32))
    return pl.pallas_call(
        kernel,
        out_shape=(jax.ShapeDtypeStruct((NC, NX, 48, 256), F32),
                   jax.ShapeDtypeStruct((NC, NX, 8, 8, 512), F32)),
        in_specs=[pl.BlockSpec(memory_space=pl.ANY)] * 2,
        out_specs=[pl.BlockSpec(memory_space=pl.ANY)] * 2,
        scratch_shapes=[
            pltpu.VMEM((4, 2, 4, 64, 1536), BF16),
            pltpu.VMEM((4, 1536, 256), BF16),
            pltpu.VMEM((512, 256), BF16),
            pltpu.VMEM((3, NZ, NY, NX, 16, 256), F32),
            pltpu.VMEM((NC, NX, 48, 256), F32),
            pltpu.VMEM((NC, NX, 8, 8, 512), F32),
            pltpu.VMEM((16, 8, 512), F32),
            pltpu.VMEM((8, 512), F32),
            pltpu.VMEM((7, 8, 512), F32),
            pltpu.SemaphoreType.DMA((8,)),
            pltpu.SemaphoreType.DMA((96,)),
            pltpu.SemaphoreType.DMA((96,)),
            pltpu.SemaphoreType.DMA((2,)),
        ] + bufs,
        compiler_params=pltpu.CompilerParams(
            collective_id=1, has_side_effects=True, vmem_limit_bytes=56 * 2**20),
    )(act, basis)


def diag_inverse(groups):
    n = len(groups)
    a = list(groups)
    sub = lax.broadcasted_iota(jnp.int32, (8, 128), 0)
    lane = lax.broadcasted_iota(jnp.int32, (8, 128), 1)
    out = []
    for s in range(n):
        c0 = 8 * s
        r = a[s]
        b = [jnp.broadcast_to(r[:, c0 + j:c0 + j + 1], (8, 128)) for j in range(8)]
        pivinv = jnp.zeros((8, 128), jnp.float32)
        for k in range(8):
            p = jnp.broadcast_to(b[k][k:k + 1, :], (8, 128))
            inv = 1.0 / p
            m = jnp.where(sub > k, b[k] * inv, 0.0)
            pivinv = jnp.where(sub == k, inv, pivinv)
            if k < 7:
                rowk = jnp.broadcast_to(r[k:k + 1, :], (8, 128))
                rowk = jnp.where(lane == c0 + k, 1.0, rowk)
                rz = jnp.where((lane == c0 + k) & (sub > k), 0.0, r)
                r = rz - m * rowk
                for j in range(k + 1, 8):
                    b[j] = b[j] - m * jnp.broadcast_to(b[j][k:k + 1, :], (8, 128))
        rel = lane - c0 - sub
        rp = jnp.where(rel == 0, 1.0, jnp.where((rel > 0) & (lane < c0 + 8), 0.0, r))
        if s + 1 < n:
            un = r * pivinv
            ut = un.T
            for t in range(s + 1, n):
                tt = ut[8 * t:8 * t + 8, :]
                acc = jnp.where((lane >= c0) & (lane < c0 + 8), 0.0, a[t])
                for k in range(8):
                    acc = acc - jnp.broadcast_to(tt[:, k:k + 1], (8, 128)) * jnp.broadcast_to(rp[k:k + 1, :], (8, 128))
                a[t] = acc
        out.append(jnp.where(lane < c0 + 8, rp, 0.0) * jnp.sqrt(pivinv))
    return out

def chol_kernel(g_ref, p_ref, o_ref, a_ref):
    K, R = 512, 192
    nb = K // 128
    for c in range(NC):
        for x in range(NX):
            a_ref[128 * x + 64 * c:128 * x + 64 * c + 64, :] = g_ref[c, x].reshape(64, K)
            a_ref[K + 48 * x:K + 48 * x + 48, 256 * c:256 * c + 256] = p_ref[c, x]
    scale = math.sqrt(1536.0)
    for b in range(nb):
        lo = 128 * b
        tiles = [a_ref[lo + 8 * i:lo + 8 * i + 8, lo:lo + 128] for i in range(16)]
        x = jnp.concatenate(diag_inverse(tiles), axis=0)
        m = lax.dot_general(a_ref[lo + 128:, lo:lo + 128], x, (((1,), (1,)), ((), ())),
                            precision=HI, preferred_element_type=F32)
        nrest = K - lo - 128
        o_ref[:, lo:lo + 128] = m[nrest:, :] * scale
        for c in range(b + 1, nb):
            off = 128 * (c - b - 1)
            a_ref[128 * c:, 128 * c:128 * c + 128] -= lax.dot_general(
                m[off:, :], m[off:off + 128, :], (((1,), (1,)), ((), ())),
                precision=HI, preferred_element_type=F32)


def chol_solve(g, p):
    return pl.pallas_call(
        chol_kernel,
        out_shape=jax.ShapeDtypeStruct((192, 512), F32),
        in_specs=[pl.BlockSpec(memory_space=pltpu.VMEM)] * 2,
        out_specs=pl.BlockSpec(memory_space=pltpu.VMEM),
        scratch_shapes=[pltpu.VMEM((704, 512), F32)],
        compiler_params=pltpu.CompilerParams(vmem_limit_bytes=32 * 2**20),
    )(g, p)


def on_device(activations, prev_basis):
    panel, gram = panel_and_gram(activations, prev_basis)
    return chol_solve(gram, panel)


def solution(mesh):
    in_specs = (P(None, ("dp", "seq"), None), P())
    out_specs = P("seq", None)
    return jax.shard_map(
        on_device, mesh=mesh, in_specs=in_specs, out_specs=out_specs, check_vma=False
    )
```

```python
import math

import jax
import jax.numpy as jnp
from jax import lax
from jax.experimental import pallas as pl
from jax.experimental.pallas import tpu as pltpu
from jax.sharding import PartitionSpec as P

F32, BF16 = jnp.float32, jnp.bfloat16
NX, NC, NZ, NY, NB = 4, 2, 8, 4, 4
HI = lax.Precision.HIGHEST
STAGES = (("z", "y", "x"), ("y", "x", "z"), ("x", "z", "y"))
SIZE = {"x": NX, "y": NY, "z": NZ}


def splat_lane(v, k):
    return jnp.broadcast_to(v[:, k:k + 1], (8, 128))


def splat_row(v, k):
    return jnp.broadcast_to(v[k:k + 1, :], (8, 128))


def diag_inverse(a, between):
    n = len(a)
    sub = lax.broadcasted_iota(jnp.int32, (8, 128), 0)
    lane = lax.broadcasted_iota(jnp.int32, (8, 128), 1)
    out = []
    col = [splat_lane(a[0], j) for j in range(8)]
    for s in range(n):
        c0 = 8 * s
        r = a[s]
        ahead = s + 1 < n
        if ahead:
            ncol = [splat_lane(a[s + 1], c0 + j) for j in range(8)]
        inv_rows = jnp.zeros((8, 128), F32)
        factors = []
        for k in range(8):
            inv = 1.0 / splat_row(col[k], k)
            inv_rows = jnp.where(sub == k, inv, inv_rows)
            m = jnp.where(sub > k, col[k] * inv, 0.0)
            if ahead:
                factors.append(ncol[k] * inv)
            if k < 7:
                row = jnp.where(lane == c0 + k, 1.0, splat_row(r, k))
                r = jnp.where((lane == c0 + k) & (sub > k), 0.0, r) - m * row
                for j in range(k + 1, 8):
                    top = splat_row(col[j], k)
                    col[j] = col[j] - m * top
                    if ahead:
                        ncol[j] = ncol[j] - factors[k] * top
        rel = lane - c0 - sub
        rp = jnp.where(rel == 0, 1.0, jnp.where((rel > 0) & (lane < c0 + 8), 0.0, r))
        out.append(jnp.where(lane < c0 + 8, rp, 0.0) * jnp.sqrt(inv_rows))
        strip = (lane >= c0) & (lane < c0 + 8)
        if ahead:
            acc = jnp.where(strip, 0.0, a[s + 1])
            for k in range(8):
                acc = acc - factors[k] * splat_row(rp, k)
            a[s + 1] = acc
            col = [splat_lane(acc, c0 + 8 + j) for j in range(8)]
        if s + 2 < n:
            ut = (r * inv_rows).T
            for t in range(s + 2, n):
                mult = ut[8 * t:8 * t + 8, :]
                acc = jnp.where(strip, 0.0, a[t])
                for k in range(8):
                    acc = acc - splat_lane(mult, k) * splat_row(rp, k)
                a[t] = acc
        between(s)
    return out


class Copies:
    def __init__(self, send_sems, recv_sems):
        self.send_sems, self.recv_sems, self.count, self.made = send_sems, recv_sems, 0, []

    def send(self, src, dst, device):
        n = self.count
        self.count += 1
        copy = pltpu.make_async_remote_copy(
            src_ref=src, dst_ref=dst, send_sem=self.send_sems.at[n], recv_sem=self.recv_sems.at[n],
            device_id=device, device_id_type=pl.DeviceIdType.MESH,
        )
        copy.start()
        self.made.append(copy)
        return copy


def ring(copies, n, me, piece, half, to, up_s, up_r, dn_s, dn_r, up_h, dn_h, up_hr, dn_hr):
    steps = n // 2
    far = piece(lax.rem(me + steps, n))
    up_h[...] = far[:half].astype(BF16)
    dn_h[...] = far[half:].astype(BF16)
    up = copies.send(up_h, up_hr, to(lax.rem(me + 1, n)))
    dn = copies.send(dn_h, dn_hr, to(lax.rem(me + n - 1, n)))
    yield
    for i in range(1, steps):
        d = steps - i
        mine = piece(lax.rem(me + d, n))
        up.wait_recv()
        if i == 1:
            up_s[0, :half] = (mine[:half] + up_hr[...].astype(F32)).astype(BF16)
            up_s[0, half:] = mine[half:].astype(BF16)
        else:
            up_s[i - 1] = (mine + up_r[i - 2].astype(F32)).astype(BF16)
        up = copies.send(up_s.at[i - 1], up_r.at[i - 1], to(lax.rem(me + 1, n)))
        mine = piece(lax.rem(me + n - d, n))
        dn.wait_recv()
        if i == 1:
            dn_s[0, half:] = (mine[half:] + dn_hr[...].astype(F32)).astype(BF16)
            dn_s[0, :half] = mine[:half].astype(BF16)
        else:
            dn_s[i - 1] = (mine + dn_r[i - 2].astype(F32)).astype(BF16)
        dn = copies.send(dn_s.at[i - 1], dn_r.at[i - 1], to(lax.rem(me + n - 1, n)))
        yield
    up.wait_recv()
    dn.wait_recv()
    return piece(me) + up_r[steps - 2].astype(F32) + dn_r[steps - 2].astype(F32)


def direct(copies, n, me, piece, to, bufs, bufr):
    sent = []
    for d in range(1, n):
        bufs[d - 1] = piece(lax.rem(me + d, n)).astype(bufs.dtype)
        sent.append(copies.send(bufs.at[d - 1], bufr.at[d - 1], to(lax.rem(me + d, n))))
    yield
    total = piece(me)
    for d in range(1, n):
        sent[d - 1].wait_recv()
        total = total + bufr[d - 1].astype(F32)
    return total


def kernel(act, basis, out, *scratch):
    (a_v, b_v, proj, pan, p_v, g_v, gs, gr, up, rows_v, out_v, load_sems, send_sems, recv_sems, out_sems,
     *bufs) = scratch
    bufs = list(bufs)
    dp, seq = lax.axis_index("dp"), lax.axis_index("seq")
    x, c, z, y = dp // 2, lax.rem(dp, 2), seq // NY, lax.rem(seq, NY)
    zz = lax.rem(z, 2)
    me = {"x": x, "y": y, "z": z}

    def dev(x_=None, c_=None, z_=None, y_=None):
        x_, c_, z_, y_ = (x if x_ is None else x_, c if c_ is None else c_,
                          z if z_ is None else z_, y if y_ is None else y_)
        return (x_ * NC + c_, z_ * NY + y_)

    peers = [dev(c_=1 - c)]
    for d in range(1, NX):
        peers.append(dev(x_=lax.rem(x + d, NX)))
    for d in range(1, NY):
        peers += [dev(y_=lax.rem(y + d, NY)), dev(z_=z + 1 - 2 * zz, y_=lax.rem(y + d, NY))]
    for d in range(1, NZ):
        peers.append(dev(z_=lax.rem(z + d, NZ)))
    barrier = pltpu.get_barrier_semaphore()
    for peer in peers:
        pl.semaphore_signal(barrier, inc=1, device_id=peer, device_id_type=pl.DeviceIdType.MESH)

    order = [lax.rem(z // 2 + o, 4) for o in (2, 1, 3, 0)]
    own_loads, b_loads = [], []
    for i, j in enumerate(order):
        cols = pl.ds(pl.multiple_of(j * 1536, 1536), 1536)
        b_loads.append(pltpu.make_async_copy(
            basis.at[j, :, pl.ds(pl.multiple_of(c * 256, 256), 256)], b_v.at[i], load_sems.at[i]))
        own_loads.append(pltpu.make_async_copy(act.at[:, :, cols], a_v.at[i, 0], load_sems.at[4 + i]))
        own_loads[i].start()
        b_loads[i].start()

    pl.semaphore_wait(barrier, len(peers))

    copies = Copies(send_sems, recv_sems)
    exchanged = []
    for i, j in enumerate(order):
        cols = pl.ds(pl.multiple_of(j * 1536, 1536), 1536)
        exchanged.append(copies.send(act.at[:, :, cols], a_v.at[i, 1], dev(c_=1 - c)))

    def first(t, sub, pool):
        axis = STAGES[t][0]
        if t == 0:
            view, pos = pan.at[0, :, 2 * sub:2 * sub + 2], 0
        else:
            view, pos = pan.at[t, pl.ds(2 * order[sub], 2)], t

        def piece(dest):
            return view[(slice(None),) * pos + (dest,)]

        def to(dest):
            return dev(**{axis + "_": dest})

        total = yield from ring(copies, SIZE[axis], me[axis], piece, 1, to, *pool[:8])
        if t == 0:
            mid[0][2 * sub:2 * sub + 2] = total
        else:
            mid[t][pl.ds(2 * order[sub], 2)] = total

    def rest(t, pool):
        left = [a for a in ("z", "y", "x") if a != STAGES[t][0]]
        cur = mid[t]
        for stage in (1, 2):
            axis = STAGES[t][stage]
            pos = left.index(axis)
            left.pop(pos)

            def piece(dest, cur=cur, pos=pos):
                return cur[(slice(None),) * pos + (dest,)]

            def to(dest, axis=axis):
                return dev(**{axis + "_": dest})

            total = yield from direct(copies, SIZE[axis], me[axis], piece, to, pool[0], pool[1])
            if stage == 1:
                cur = pool[2]
                cur[...] = total
                pool = pool[3:]
            else:
                p_v[c, x, 16 * t:16 * t + 16, :] = total * (1.0 / 65536.0)

    mid = [bufs.pop(0) for _ in range(3)]
    rings = []
    for t in range(3):
        subs = []
        for sub in range(2 if t == 0 else 4):
            subs.append(first(t, sub, bufs[:8]))
            bufs = bufs[8:]
        rings.append(subs)
    rests = []
    for t in range(3):
        rests.append(rest(t, bufs[:5]))
        bufs = bufs[5:]

    def step(gen):
        try:
            next(gen)
            return True
        except StopIteration:
            return False

    def compute(i):
        j = order[i]
        b_loads[i].wait()
        own_loads[i].wait()
        proj[0:256, :] = jnp.dot(a_v[i, 0].reshape(256, 1536), b_v[i], preferred_element_type=F32).astype(BF16)
        exchanged[i].wait_recv()
        proj[256:512, :] = jnp.dot(a_v[i, 1].reshape(256, 1536), b_v[i], preferred_element_type=F32).astype(BF16)
        for k in range(4):
            lhs = a_v[i, :, :, :, 384 * k:384 * k + 384].reshape(512, 384)
            r = lax.dot_general(lhs, proj[...], (((0,), (0,)), ((), ())), preferred_element_type=F32)
            r = r.reshape(2, 4, 3, 16, 256)
            for t in range(3):
                pan[t, 2 * j + k // 2, 2 * (k % 2):2 * (k % 2) + 2] = r[:, :, t]

    compute(0)
    step(rings[0][0])
    step(rings[0][1])
    step(rings[1][0])
    step(rings[2][0])
    compute(1)
    step(rings[1][1])
    step(rings[2][1])
    compute(2)
    step(rings[1][2])
    step(rings[2][2])
    step(rings[0][0])
    step(rings[0][1])
    step(rings[1][0])
    step(rings[2][0])
    compute(3)
    step(rings[1][3])
    step(rings[2][3])
    step(rings[1][1])
    step(rings[2][1])
    step(rings[0][0])
    step(rings[0][1])
    step(rings[1][2])
    step(rings[2][2])
    step(rings[1][0])
    step(rings[2][0])
    step(rings[0][0])
    step(rings[0][1])
    step(rings[1][3])
    step(rings[2][3])
    for sub in range(1, 4):
        step(rings[1][sub])
        step(rings[2][sub])
    step(rests[2])
    step(rests[1])
    step(rings[0][0])
    step(rings[0][1])
    step(rests[0])

    step(rests[1])
    step(rests[0])
    step(rests[2])
    step(rests[0])
    step(rests[1])
    step(rests[2])

    sent = []
    for d in range(1, NX):
        sent.append(copies.send(p_v.at[c, x], p_v.at[c, x], dev(x_=lax.rem(x + d, NX))))
    swap = copies.send(p_v.at[c, x], p_v.at[c, x], dev(c_=1 - c))
    passed = [swap]
    for d in range(1, NX):
        sent[d - 1].wait_recv()
        other = lax.rem(x + NX - d, NX)
        passed.append(copies.send(p_v.at[c, other], p_v.at[c, other], dev(c_=1 - c)))
    for copy in passed:
        copy.wait_recv()

    for h in range(2):
        rows_v[:, 256 * h:256 * h + 256] = p_v[h].reshape(192, 256)
    for b in range(NB):
        lo = 128 * b
        gs[b, :, :, :, lo:] = lax.dot_general(
            rows_v[:, lo:lo + 128], rows_v[:, lo:], (((0,), (0,)), ((), ())), precision=HI,
            preferred_element_type=F32).reshape(8, 2, 8, 512 - lo)
    q_me = c * NX + x
    p_me = zz * NY + y
    parts = (pl.ds(0, 1), pl.ds(1, NB - 1))

    def peer(d):
        q = lax.rem(p_me + d, 8)
        return q, dev(z_=z - zz + q // NY, y_=lax.rem(q, NY))

    def cols(p):
        return pl.ds(pl.multiple_of(lax.rem(p, NB) * 128, 128), 128)

    reduced = [[], []]
    for h, part in enumerate(parts):
        for d in range(1, 8):
            p, to = peer(d)
            reduced[h].append(copies.send(
                gs.at[part, q_me, p // NB, :, cols(p)], gr.at[d - 1, part], to))
    spread = [[], []]
    for h, part in enumerate(parts):
        total = gs[part, q_me, p_me // NB, :, cols(p_me)]
        for d in range(1, 8):
            reduced[h][d - 1].wait_recv()
            total = total + gr[d - 1, part]
        g_v[part, c, x, p_me] = total
        for d in range(1, 8):
            mine = g_v.at[part, c, x, p_me]
            spread[h].append(copies.send(mine, mine, peer(d)[1]))
    across = [[], []]
    for h, part in enumerate(parts):
        for copy in spread[h]:
            copy.wait_recv()
        for d in range(1, NX):
            mine = g_v.at[part, c, x]
            across[h].append(copies.send(mine, mine, dev(x_=lax.rem(x + d, NX))))
    swapped = [None, None]

    def swap_cores(h):
        for copy in across[h]:
            copy.wait_recv()
        mine = g_v.at[parts[h], c]
        swapped[h] = copies.send(mine, mine, dev(c_=1 - c))

    def arrive(h):
        swapped[h].wait_recv()
        for b in range(1) if h == 0 else range(1, NB):
            for q in range(8):
                for rt in range(2):
                    for ct in range(b, NB):
                        up[b, 16 * q + 8 * rt:16 * q + 8 * rt + 8, 128 * ct:128 * ct + 128] = (
                            g_v[b, q // NX, q % NX, NB * rt + ct])

    swap_cores(0)
    arrive(0)
    written = []
    for b in range(NB):
        lo, hi = 128 * b, 128 * b + 128

        def between(strip):
            if b == 0 and strip == 7:
                swap_cores(1)

        inv = jnp.concatenate(
            diag_inverse([up[b, 8 * i:8 * i + 8, lo:hi] for i in range(16)], between), axis=0)
        if b == 0:
            arrive(1)
        if b < NB - 1:
            u = jnp.dot(inv, up[b, :, hi:], precision=HI, preferred_element_type=F32)
            for e in range(b + 1, NB):
                off = 128 * (e - b - 1)
                up[e, :, 128 * e:] -= lax.dot_general(
                    u[:, off:off + 128], u[:, off:], (((0,), (0,)), ((), ())), precision=HI,
                    preferred_element_type=F32)
        solved = lax.dot_general(rows_v[:, lo:hi], inv, (((1,), (1,)), ((), ())), precision=HI,
                                 preferred_element_type=F32)
        out_v[:, lo:hi] = solved * math.sqrt(1536.0)
        written.append(pltpu.make_async_copy(out_v.at[:, lo:hi], out.at[:, lo:hi], out_sems.at[b]))
        written[b].start()
        if b < NB - 1:
            rows_v[:, hi:] -= jnp.dot(solved, u, precision=HI, preferred_element_type=F32)
    for copy in copies.made:
        copy.wait_send()
    for copy in written:
        copy.wait()


def refreshed(act, basis):
    tile = (16, 256)
    mids, firsts, rests = [], [], []
    for t, axes in enumerate(STAGES):
        left = [a for a in ("z", "y", "x") if a != axes[0]]
        mids.append(pltpu.VMEM(tuple(SIZE[a] for a in left) + tile, F32))
        steps = SIZE[axes[0]] // 2
        full = (2, 4) + tile
        for _ in range(2 if t == 0 else 4):
            firsts += [pltpu.VMEM((steps - 1,) + full, BF16)] * 4 + [pltpu.VMEM((1,) + full[1:], BF16)] * 4
        left.remove(axes[1])
        shape = (SIZE[left[0]],) + tile
        rests += [pltpu.VMEM((SIZE[axes[1]] - 1,) + shape, BF16)] * 2 + [pltpu.VMEM(shape, F32)]
        rests += [pltpu.VMEM((SIZE[axes[2]] - 1,) + tile, F32)] * 2
    bufs = mids + firsts + rests
    return pl.pallas_call(
        kernel,
        out_shape=jax.ShapeDtypeStruct((192, 512), F32),
        in_specs=[pl.BlockSpec(memory_space=pl.ANY)] * 2,
        out_specs=pl.BlockSpec(memory_space=pl.ANY),
        scratch_shapes=[
            pltpu.VMEM((4, 2, 4, 64, 1536), BF16),
            pltpu.VMEM((4, 1536, 256), BF16),
            pltpu.VMEM((512, 256), BF16),
            pltpu.VMEM((3, NZ, NY, NX, 16, 256), F32),
            pltpu.VMEM((NC, NX, 48, 256), F32),
            pltpu.VMEM((NB, NC, NX, 8, 8, 128), F32),
            pltpu.VMEM((NB, 8, 2, 8, 512), F32),
            pltpu.VMEM((7, NB, 8, 128), F32),
            pltpu.VMEM((NB, 128, 512), F32),
            pltpu.VMEM((192, 512), F32),
            pltpu.VMEM((192, 512), F32),
            pltpu.SemaphoreType.DMA((8,)),
            pltpu.SemaphoreType.DMA((128,)),
            pltpu.SemaphoreType.DMA((128,)),
            pltpu.SemaphoreType.DMA((4,)),
        ] + bufs,
        compiler_params=pltpu.CompilerParams(
            collective_id=1, has_side_effects=True, vmem_limit_bytes=56 * 2**20),
    )(act, basis)


def on_device(activations, prev_basis):
    return refreshed(activations, prev_basis)


def solution(mesh):
    in_specs = (P(None, ("dp", "seq"), None), P())
    out_specs = P("seq", None)
    return jax.shard_map(
        on_device, mesh=mesh, in_specs=in_specs, out_specs=out_specs, check_vma=False
    )
```

```python
import functools
import math

import jax
import jax.numpy as jnp
from jax import lax
from jax.experimental import pallas as pl
from jax.experimental.pallas import tpu as pltpu
from jax.sharding import PartitionSpec as P

F32, BF16 = jnp.float32, jnp.bfloat16
NX, NC, NZ, NY, NB = 4, 2, 8, 4, 4
HI = lax.Precision.HIGHEST
STAGES = (("z", "y", "x"), ("y", "x", "z"), ("x", "y", "z"))
SIZE = {"x": NX, "y": NY, "z": NZ}


def splat_lane(v, k):
    return jnp.broadcast_to(v[:, k:k + 1], (8, 128))


def splat_row(v, k):
    return jnp.broadcast_to(v[k:k + 1, :], (8, 128))


def three_terms(v):
    high = v.astype(BF16).astype(F32)
    left = v - high
    middle = left.astype(BF16).astype(F32)
    return high, middle, left - middle


def diag_inverse(a, between):
    n = len(a)
    sub = lax.broadcasted_iota(jnp.int32, (8, 128), 0)
    lane = lax.broadcasted_iota(jnp.int32, (8, 128), 1)
    out = []
    col = [splat_lane(a[0], j) for j in range(8)]
    for s in range(n):
        c0 = 8 * s
        r = a[s]
        ahead = s + 1 < n
        if ahead:
            ncol = [splat_lane(a[s + 1], c0 + j) for j in range(8)]
        inv_rows = jnp.zeros((8, 128), F32)
        factors = []
        for k in range(8):
            inv = 1.0 / splat_row(col[k], k)
            inv_rows = jnp.where(sub == k, inv, inv_rows)
            m = jnp.where(sub > k, col[k] * inv, 0.0)
            if ahead:
                factors.append(ncol[k] * inv)
            if k < 7:
                row = jnp.where(lane == c0 + k, 1.0, splat_row(r, k))
                r = jnp.where((lane == c0 + k) & (sub > k), 0.0, r) - m * row
                for j in range(k + 1, 8):
                    top = splat_row(col[j], k)
                    col[j] = col[j] - m * top
                    if ahead:
                        ncol[j] = ncol[j] - factors[k] * top
        rel = lane - c0 - sub
        rp = jnp.where(rel == 0, 1.0, jnp.where((rel > 0) & (lane < c0 + 8), 0.0, r))
        out.append(jnp.where(lane < c0 + 8, rp, 0.0) * jnp.sqrt(inv_rows))
        strip = (lane >= c0) & (lane < c0 + 8)
        if ahead:
            acc = jnp.where(strip, 0.0, a[s + 1])
            for k in range(8):
                acc = acc - factors[k] * splat_row(rp, k)
            a[s + 1] = acc
            col = [splat_lane(acc, c0 + 8 + j) for j in range(8)]
        if s + 2 < n:
            uh, um, ul = three_terms(r * inv_rows)
            rh, rm, rl = three_terms(rp)
            left = jnp.concatenate([uh, uh, um, uh, ul, um], axis=0).astype(BF16)
            right = jnp.concatenate([rh, rm, rh, rl, rh, rm], axis=0).astype(BF16)
            update = lax.dot_general(left, right, (((0,), (0,)), ((), ())), preferred_element_type=F32)
            for t in range(s + 2, n):
                a[t] = jnp.where(strip, 0.0, a[t]) - update[8 * t:8 * t + 8, :]
        between(s)
    return out


class Copies:
    def __init__(self, send_sems, recv_sems):
        self.send_sems, self.recv_sems, self.count, self.made = send_sems, recv_sems, 0, []

    def send(self, src, dst, device):
        n = self.count
        self.count += 1
        copy = pltpu.make_async_remote_copy(
            src_ref=src, dst_ref=dst, send_sem=self.send_sems.at[n], recv_sem=self.recv_sems.at[n],
            device_id=device, device_id_type=pl.DeviceIdType.MESH,
        )
        copy.start()
        self.made.append(copy)
        return copy


def ring(copies, n, me, piece, half, to, up_s, up_r, dn_s, dn_r, up_h, dn_h, up_hr, dn_hr):
    steps = n // 2
    far = piece(lax.rem(me + steps, n))
    up_h[...] = far[:half].astype(BF16)
    dn_h[...] = far[half:].astype(BF16)
    up = copies.send(up_h, up_hr, to(lax.rem(me + 1, n)))
    dn = copies.send(dn_h, dn_hr, to(lax.rem(me + n - 1, n)))
    yield
    for i in range(1, steps):
        d = steps - i
        mine = piece(lax.rem(me + d, n))
        up.wait_recv()
        if i == 1:
            up_s[0, :half] = (mine[:half] + up_hr[...].astype(F32)).astype(BF16)
            up_s[0, half:] = mine[half:].astype(BF16)
        else:
            up_s[i - 1] = (mine + up_r[i - 2].astype(F32)).astype(BF16)
        up = copies.send(up_s.at[i - 1], up_r.at[i - 1], to(lax.rem(me + 1, n)))
        mine = piece(lax.rem(me + n - d, n))
        dn.wait_recv()
        if i == 1:
            dn_s[0, half:] = (mine[half:] + dn_hr[...].astype(F32)).astype(BF16)
            dn_s[0, :half] = mine[:half].astype(BF16)
        else:
            dn_s[i - 1] = (mine + dn_r[i - 2].astype(F32)).astype(BF16)
        dn = copies.send(dn_s.at[i - 1], dn_r.at[i - 1], to(lax.rem(me + n - 1, n)))
        yield
    up.wait_recv()
    dn.wait_recv()
    return piece(me) + up_r[steps - 2].astype(F32) + dn_r[steps - 2].astype(F32)


def direct(copies, n, me, piece, to, bufs, bufr):
    sent = []
    for d in range(1, n):
        bufs[d - 1] = piece(lax.rem(me + d, n)).astype(bufs.dtype)
        sent.append(copies.send(bufs.at[d - 1], bufr.at[d - 1], to(lax.rem(me + d, n))))
    yield
    total = piece(me)
    for d in range(1, n):
        sent[d - 1].wait_recv()
        total = total + bufr[d - 1].astype(F32)
    return total


def kernel(act, basis, out, *scratch):
    (a_v, b_v, proj, pan, p_v, g_v, gs, gr, up, rows_v, out_v, load_sems, send_sems, recv_sems, out_sems,
     *bufs) = scratch
    bufs = list(bufs)
    dp, seq = lax.axis_index("dp"), lax.axis_index("seq")
    x, c, z, y = dp // 2, lax.rem(dp, 2), seq // NY, lax.rem(seq, NY)
    zz = lax.rem(z, 2)
    me = {"x": x, "y": y, "z": z}

    def dev(x_=None, c_=None, z_=None, y_=None):
        x_, c_, z_, y_ = (x if x_ is None else x_, c if c_ is None else c_,
                          z if z_ is None else z_, y if y_ is None else y_)
        return (x_ * NC + c_, z_ * NY + y_)

    peers = [dev(c_=1 - c)]
    for d in range(1, NX):
        peers.append(dev(x_=lax.rem(x + d, NX)))
    for d in range(1, NY):
        peers += [dev(y_=lax.rem(y + d, NY)), dev(z_=z + 1 - 2 * zz, y_=lax.rem(y + d, NY))]
    for d in range(1, NZ):
        peers.append(dev(z_=lax.rem(z + d, NZ)))
    barrier = pltpu.get_barrier_semaphore()
    for peer in peers:
        pl.semaphore_signal(barrier, inc=1, device_id=peer, device_id_type=pl.DeviceIdType.MESH)

    order = [lax.rem(z // 2 + o, 4) for o in (2, 1, 3, 0)]
    own_loads, b_loads = [], []
    for i, j in enumerate(order):
        cols = pl.ds(pl.multiple_of(j * 1536, 1536), 1536)
        b_loads.append(pltpu.make_async_copy(
            basis.at[j, :, pl.ds(pl.multiple_of(c * 256, 256), 256)], b_v.at[i], load_sems.at[i]))
        own_loads.append(pltpu.make_async_copy(act.at[:, :, cols], a_v.at[i, 0], load_sems.at[4 + i]))
        own_loads[i].start()
        b_loads[i].start()

    pl.semaphore_wait(barrier, len(peers))

    copies = Copies(send_sems, recv_sems)
    exchanged = []
    for i, j in enumerate(order):
        cols = pl.ds(pl.multiple_of(j * 1536, 1536), 1536)
        exchanged.append(copies.send(act.at[:, :, cols], a_v.at[i, 1], dev(c_=1 - c)))

    def first(t, sub, pool):
        axis = STAGES[t][0]
        if t == 0:
            view, pos = pan.at[0, :, 2 * sub:2 * sub + 2], 0
        else:
            view, pos = pan.at[t, pl.ds(2 * order[sub], 2)], t

        def piece(dest):
            return view[(slice(None),) * pos + (dest,)]

        def to(dest):
            return dev(**{axis + "_": dest})

        total = yield from ring(copies, SIZE[axis], me[axis], piece, 1, to, *pool[:8])
        if t == 0:
            mid[0][2 * sub:2 * sub + 2] = total
        else:
            mid[t][pl.ds(2 * order[sub], 2)] = total

    def rest(t, pool):
        left = [a for a in ("z", "y", "x") if a != STAGES[t][0]]
        cur = mid[t]
        for stage in (1, 2):
            axis = STAGES[t][stage]
            pos = left.index(axis)
            left.pop(pos)

            def piece(dest, cur=cur, pos=pos):
                return cur[(slice(None),) * pos + (dest,)]

            def to(dest, axis=axis):
                return dev(**{axis + "_": dest})

            total = yield from direct(copies, SIZE[axis], me[axis], piece, to, pool[0], pool[1])
            if stage == 1:
                cur = pool[2]
                cur[...] = total
                pool = pool[3:]
            else:
                p_v[c, x, 16 * t:16 * t + 16, :] = total * (1.0 / 65536.0)

    mid = [bufs.pop(0) for _ in range(3)]
    rings = []
    for t in range(3):
        subs = []
        for sub in range(2 if t == 0 else 4):
            subs.append(first(t, sub, bufs[:8]))
            bufs = bufs[8:]
        rings.append(subs)
    rests = []
    for t in range(3):
        rests.append(rest(t, bufs[:5]))
        bufs = bufs[5:]

    def step(gen):
        try:
            next(gen)
            return True
        except StopIteration:
            return False

    def compute(i):
        j = order[i]
        b_loads[i].wait()
        own_loads[i].wait()
        proj[0:256, :] = jnp.dot(a_v[i, 0].reshape(256, 1536), b_v[i], preferred_element_type=F32).astype(BF16)
        exchanged[i].wait_recv()
        proj[256:512, :] = jnp.dot(a_v[i, 1].reshape(256, 1536), b_v[i], preferred_element_type=F32).astype(BF16)
        for k in range(4):
            lhs = a_v[i, :, :, :, 384 * k:384 * k + 384].reshape(512, 384)
            r = lax.dot_general(lhs, proj[...], (((0,), (0,)), ((), ())), preferred_element_type=F32)
            r = r.reshape(2, 4, 3, 16, 256)
            for t in range(3):
                pan[t, 2 * j + k // 2, 2 * (k % 2):2 * (k % 2) + 2] = r[:, :, t]

    compute(0)
    step(rings[0][0])
    step(rings[0][1])
    step(rings[1][0])
    step(rings[2][0])
    compute(1)
    step(rings[1][1])
    step(rings[2][1])
    compute(2)
    step(rings[1][2])
    step(rings[2][2])
    step(rings[0][0])
    step(rings[0][1])
    step(rings[1][0])
    step(rings[2][0])
    compute(3)
    step(rings[1][3])
    step(rings[2][3])
    step(rings[1][1])
    step(rings[2][1])
    step(rings[0][0])
    step(rings[0][1])
    step(rings[1][2])
    step(rings[2][2])
    step(rings[1][0])
    step(rings[2][0])
    step(rings[0][0])
    step(rings[0][1])
    step(rings[1][3])
    step(rings[2][3])
    for sub in range(1, 4):
        step(rings[1][sub])
        step(rings[2][sub])
    step(rests[2])
    step(rests[1])
    step(rings[0][0])
    step(rings[0][1])
    step(rests[0])
    step(rests[1])
    step(rests[2])
    step(rests[0])
    step(rests[1])
    step(rests[2])
    step(rests[0])

    sent = []
    for d in range(1, NX):
        sent.append(copies.send(p_v.at[c, x], p_v.at[c, x], dev(x_=lax.rem(x + d, NX))))
    swap = copies.send(p_v.at[c, x], p_v.at[c, x], dev(c_=1 - c))
    passed = [swap]
    for d in range(1, NX):
        sent[d - 1].wait_recv()
        other = lax.rem(x + NX - d, NX)
        passed.append(copies.send(p_v.at[c, other], p_v.at[c, other], dev(c_=1 - c)))
    for copy in passed:
        copy.wait_recv()

    for h in range(2):
        rows_v[:, 256 * h:256 * h + 256] = p_v[h].reshape(192, 256)
    def gram(b):
        lo = 128 * b
        gs[b, :, :, :, lo:] = lax.dot_general(
            rows_v[:, lo:lo + 128], rows_v[:, lo:], (((0,), (0,)), ((), ())), precision=HI,
            preferred_element_type=F32).reshape(8, 2, 8, 512 - lo)

    q_me = c * NX + x
    p_me = zz * NY + y
    parts = (pl.ds(0, 1), pl.ds(1, NB - 1))

    def peer(d):
        q = lax.rem(p_me + d, 8)
        return q, dev(z_=z - zz + q // NY, y_=lax.rem(q, NY))

    def cols(p):
        return pl.ds(pl.multiple_of(lax.rem(p, NB) * 128, 128), 128)

    reduced = [[], []]
    for h, part in enumerate(parts):
        for b in range(1) if h == 0 else range(1, NB):
            gram(b)
        for d in range(1, 8):
            p, to = peer(d)
            reduced[h].append(copies.send(
                gs.at[part, q_me, p // NB, :, cols(p)], gr.at[d - 1, part], to))
    spread = [[], []]
    for h, part in enumerate(parts):
        total = gs[part, q_me, p_me // NB, :, cols(p_me)]
        for d in range(1, 8):
            reduced[h][d - 1].wait_recv()
            total = total + gr[d - 1, part]
        g_v[part, c, x, p_me // NB, lax.rem(p_me, NB)] = total
        for d in range(1, 8):
            mine = g_v.at[part, c, x, p_me // NB, lax.rem(p_me, NB)]
            spread[h].append(copies.send(mine, mine, peer(d)[1]))
    diagonal, across, swapped = [], [[] for _ in range(NB)], []

    def spread_x(b):
        for d in range(1, NX):
            mine = g_v.at[b, c, x, :, max(b, 1):]
            across[b].append(copies.send(mine, mine, dev(x_=lax.rem(x + d, NX))))

    for copy in spread[0]:
        copy.wait_recv()
    for d in range(1, 8):
        mine = g_v.at[0, c, x, :, 0]
        diagonal.append(copies.send(
            mine, mine, dev(x_=lax.rem(x + d // 2, NX), c_=c if d % 2 == 0 else 1 - c)))
    spread_x(0)
    for copy in spread[1]:
        copy.wait_recv()
    for b in range(1, NB):
        spread_x(b)

    def swap_cores(b):
        for copy in across[b]:
            copy.wait_recv()
        mine = g_v.at[b, c, :, :, max(b, 1):]
        swapped.append(copies.send(mine, mine, dev(c_=1 - c)))

    def take(b, first, last):
        for q in range(8):
            for rt in range(2):
                for ct in range(first, last):
                    up[b, 16 * q + 8 * rt:16 * q + 8 * rt + 8, 128 * ct:128 * ct + 128] = (
                        g_v[b, q // NX, q % NX, rt, ct])

    def arrive(b):
        swapped[b].wait_recv()
        take(b, max(b, 1), NB)

    for copy in diagonal:
        copy.wait_recv()
    take(0, 0, 1)
    for b in range(NB):
        lo, hi = 128 * b, 128 * b + 128

        def between(strip):
            if b == 0 and strip in (3, 5, 8, 9):
                swap_cores((3, 5, 8, 9).index(strip))

        inv = jnp.concatenate(
            diag_inverse([up[b, 8 * i:8 * i + 8, lo:hi] for i in range(16)], between), axis=0)
        if b == 0:
            for e in range(NB):
                arrive(e)
        if b < NB - 1:
            u = jnp.dot(inv, up[b, :, hi:], precision=HI, preferred_element_type=F32)
            for e in range(b + 1, NB):
                off = 128 * (e - b - 1)
                up[e, :, 128 * e:] -= lax.dot_general(
                    u[:, off:off + 128], u[:, off:], (((0,), (0,)), ((), ())), precision=HI,
                    preferred_element_type=F32)
        solved = lax.dot_general(rows_v[:, lo:hi], inv, (((1,), (1,)), ((), ())), precision=HI,
                                 preferred_element_type=F32)
        out_v[:, lo:hi] = solved * math.sqrt(1536.0)
        if b < NB - 1:
            rows_v[:, hi:] -= jnp.dot(solved, u, precision=HI, preferred_element_type=F32)
    written = pltpu.make_async_copy(out_v, out, out_sems.at[0])
    written.start()
    for copy in copies.made:
        copy.wait_send()
    written.wait()


def refreshed(act, basis):
    tile = (16, 256)
    mids, firsts, rests = [], [], []
    for t, axes in enumerate(STAGES):
        left = [a for a in ("z", "y", "x") if a != axes[0]]
        mids.append(pltpu.VMEM(tuple(SIZE[a] for a in left) + tile, F32))
        steps = SIZE[axes[0]] // 2
        full = (2, 4) + tile
        for _ in range(2 if t == 0 else 4):
            firsts += [pltpu.VMEM((steps - 1,) + full, BF16)] * 4 + [pltpu.VMEM((1,) + full[1:], BF16)] * 4
        left.remove(axes[1])
        shape = (SIZE[left[0]],) + tile
        rests += [pltpu.VMEM((SIZE[axes[1]] - 1,) + shape, BF16)] * 2 + [pltpu.VMEM(shape, F32)]
        rests += [pltpu.VMEM((SIZE[axes[2]] - 1,) + tile, F32)] * 2
    bufs = mids + firsts + rests
    return pl.pallas_call(
        kernel,
        out_shape=jax.ShapeDtypeStruct((192, 512), F32),
        in_specs=[pl.BlockSpec(memory_space=pl.ANY)] * 2,
        out_specs=pl.BlockSpec(memory_space=pl.ANY),
        scratch_shapes=[
            pltpu.VMEM((4, 2, 4, 64, 1536), BF16),
            pltpu.VMEM((4, 1536, 256), BF16),
            pltpu.VMEM((512, 256), BF16),
            pltpu.VMEM((3, NZ, NY, NX, 16, 256), F32),
            pltpu.VMEM((NC, NX, 48, 256), F32),
            pltpu.VMEM((NB, NC, NX, 2, NB, 8, 128), F32),
            pltpu.VMEM((NB, 8, 2, 8, 512), F32),
            pltpu.VMEM((7, NB, 8, 128), F32),
            pltpu.VMEM((NB, 128, 512), F32),
            pltpu.VMEM((192, 512), F32),
            pltpu.VMEM((192, 512), F32),
            pltpu.SemaphoreType.DMA((8,)),
            pltpu.SemaphoreType.DMA((192,)),
            pltpu.SemaphoreType.DMA((192,)),
            pltpu.SemaphoreType.DMA((1,)),
        ] + bufs,
        compiler_params=pltpu.CompilerParams(
            collective_id=1, has_side_effects=True, vmem_limit_bytes=56 * 2**20),
    )(act, basis)


def on_device(activations, prev_basis):
    return refreshed(activations, prev_basis)


def solution(mesh):
    in_specs = (P(None, ("dp", "seq"), None), P())
    out_specs = P("seq", None)
    return jax.shard_map(
        on_device, mesh=mesh, in_specs=in_specs, out_specs=out_specs, check_vma=False
    )
```

```python
import functools
import math

import jax
import jax.numpy as jnp
from jax import lax
from jax.experimental import pallas as pl
from jax.experimental.pallas import tpu as pltpu
from jax.sharding import PartitionSpec as P

F32, BF16 = jnp.float32, jnp.bfloat16
NX, NC, NZ, NY, NB = 4, 2, 8, 4, 4
HI = lax.Precision.HIGHEST
STAGES = (("z", "y", "x"), ("y", "x", "z"), ("x", "y", "z"))
SIZE = {"x": NX, "y": NY, "z": NZ}


def splat_lane(v, k):
    return jnp.broadcast_to(v[:, k:k + 1], (8, 128))


def splat_row(v, k):
    return jnp.broadcast_to(v[k:k + 1, :], (8, 128))


def three_terms(v):
    high = v.astype(BF16).astype(F32)
    left = v - high
    middle = left.astype(BF16).astype(F32)
    return high, middle, left - middle


def diag_inverse(a, between):
    n = len(a)
    sub = lax.broadcasted_iota(jnp.int32, (8, 128), 0)
    lane = lax.broadcasted_iota(jnp.int32, (8, 128), 1)
    out = []
    col = [splat_lane(a[0], j) for j in range(8)]
    for s in range(n):
        c0 = 8 * s
        r = a[s]
        ahead = s + 1 < n
        if ahead:
            ncol = [splat_lane(a[s + 1], c0 + j) for j in range(8)]
        inv_rows = jnp.zeros((8, 128), F32)
        factors = []
        for k in range(8):
            inv = 1.0 / splat_row(col[k], k)
            inv_rows = jnp.where(sub == k, inv, inv_rows)
            m = jnp.where(sub > k, col[k] * inv, 0.0)
            if ahead:
                factors.append(ncol[k] * inv)
            if k < 7:
                row = jnp.where(lane == c0 + k, 1.0, splat_row(r, k))
                r = jnp.where((lane == c0 + k) & (sub > k), 0.0, r) - m * row
                for j in range(k + 1, 8):
                    top = splat_row(col[j], k)
                    col[j] = col[j] - m * top
                    if ahead:
                        ncol[j] = ncol[j] - factors[k] * top
        rel = lane - c0 - sub
        rp = jnp.where(rel == 0, 1.0, jnp.where((rel > 0) & (lane < c0 + 8), 0.0, r))
        out.append(jnp.where(lane < c0 + 8, rp, 0.0) * jnp.sqrt(inv_rows))
        strip = (lane >= c0) & (lane < c0 + 8)
        if ahead:
            acc = jnp.where(strip, 0.0, a[s + 1])
            for k in range(8):
                acc = acc - factors[k] * splat_row(rp, k)
            a[s + 1] = acc
            col = [splat_lane(acc, c0 + 8 + j) for j in range(8)]
        if s + 2 < n:
            uh, um, ul = three_terms(r * inv_rows)
            rh, rm, rl = three_terms(rp)
            left = jnp.concatenate([uh, uh, um, uh, ul, um], axis=0).astype(BF16)
            right = jnp.concatenate([rh, rm, rh, rl, rh, rm], axis=0).astype(BF16)
            update = lax.dot_general(left, right, (((0,), (0,)), ((), ())), preferred_element_type=F32)
            for t in range(s + 2, n):
                a[t] = jnp.where(strip, 0.0, a[t]) - update[8 * t:8 * t + 8, :]
        between(s)
    return out


class Copies:
    def __init__(self, send_sems, recv_sems):
        self.send_sems, self.recv_sems, self.count, self.made = send_sems, recv_sems, 0, []

    def take(self, number):
        self.count += number
        return self.count - number

    def make(self, src, dst, device, n):
        return pltpu.make_async_remote_copy(
            src_ref=src, dst_ref=dst, send_sem=self.send_sems.at[n], recv_sem=self.recv_sems.at[n],
            device_id=device, device_id_type=pl.DeviceIdType.MESH,
        )

    def send(self, src, dst, device):
        copy = self.make(src, dst, device, self.take(1))
        copy.start()
        self.made.append(copy)
        return copy


def ring(copies, n, me, piece, half, to, up_s, up_r, dn_s, dn_r, up_h, dn_h, up_hr, dn_hr):
    steps = n // 2
    far = piece(lax.rem(me + steps, n))
    up_h[...] = far[:half].astype(BF16)
    dn_h[...] = far[half:].astype(BF16)
    up = copies.send(up_h, up_hr, to(lax.rem(me + 1, n)))
    dn = copies.send(dn_h, dn_hr, to(lax.rem(me + n - 1, n)))
    yield
    for i in range(1, steps):
        d = steps - i
        mine = piece(lax.rem(me + d, n))
        up.wait_recv()
        if i == 1:
            up_s[0, :half] = (mine[:half] + up_hr[...].astype(F32)).astype(BF16)
            up_s[0, half:] = mine[half:].astype(BF16)
        else:
            up_s[i - 1] = (mine + up_r[i - 2].astype(F32)).astype(BF16)
        up = copies.send(up_s.at[i - 1], up_r.at[i - 1], to(lax.rem(me + 1, n)))
        mine = piece(lax.rem(me + n - d, n))
        dn.wait_recv()
        if i == 1:
            dn_s[0, half:] = (mine[half:] + dn_hr[...].astype(F32)).astype(BF16)
            dn_s[0, :half] = mine[:half].astype(BF16)
        else:
            dn_s[i - 1] = (mine + dn_r[i - 2].astype(F32)).astype(BF16)
        dn = copies.send(dn_s.at[i - 1], dn_r.at[i - 1], to(lax.rem(me + n - 1, n)))
        yield
    up.wait_recv()
    dn.wait_recv()
    return piece(me) + up_r[steps - 2].astype(F32) + dn_r[steps - 2].astype(F32)


def direct(copies, n, me, piece, to, bufs, bufr):
    sent = []
    for d in range(1, n):
        bufs[d - 1] = piece(lax.rem(me + d, n)).astype(bufs.dtype)
        sent.append(copies.send(bufs.at[d - 1], bufr.at[d - 1], to(lax.rem(me + d, n))))
    yield
    total = piece(me)
    for d in range(1, n):
        sent[d - 1].wait_recv()
        total = total + bufr[d - 1].astype(F32)
    return total


def kernel(act, basis, out, *scratch):
    (a_v, b_v, proj, pan, p_v, g_v, gs, gr, up, rows_v, out_v, load_sems, send_sems, recv_sems, out_sems,
     *bufs) = scratch
    bufs = list(bufs)
    dp, seq = lax.axis_index("dp"), lax.axis_index("seq")
    x, c, z, y = dp // 2, lax.rem(dp, 2), seq // NY, lax.rem(seq, NY)
    zz = lax.rem(z, 2)
    me = {"x": x, "y": y, "z": z}

    def dev(x_=None, c_=None, z_=None, y_=None):
        x_, c_, z_, y_ = (x if x_ is None else x_, c if c_ is None else c_,
                          z if z_ is None else z_, y if y_ is None else y_)
        return (x_ * NC + c_, z_ * NY + y_)

    peers = [dev(c_=1 - c)]
    for d in range(1, NX):
        peers.append(dev(x_=lax.rem(x + d, NX)))
    for d in range(1, NY):
        peers += [dev(y_=lax.rem(y + d, NY)), dev(z_=z + 1 - 2 * zz, y_=lax.rem(y + d, NY))]
    for d in range(1, NZ):
        peers.append(dev(z_=lax.rem(z + d, NZ)))
    barrier = pltpu.get_barrier_semaphore()
    for peer in peers:
        pl.semaphore_signal(barrier, inc=1, device_id=peer, device_id_type=pl.DeviceIdType.MESH)

    order = [lax.rem(z // 2 + o, 4) for o in (2, 1, 3, 0)]
    own_loads, b_loads = [], []
    for i, j in enumerate(order):
        cols = pl.ds(pl.multiple_of(j * 1536, 1536), 1536)
        b_loads.append(pltpu.make_async_copy(
            basis.at[j, :, pl.ds(pl.multiple_of(c * 256, 256), 256)], b_v.at[i], load_sems.at[i]))
        own_loads.append(pltpu.make_async_copy(act.at[:, :, cols], a_v.at[i, 0], load_sems.at[4 + i]))
        own_loads[i].start()
        b_loads[i].start()

    pl.semaphore_wait(barrier, len(peers))

    copies = Copies(send_sems, recv_sems)
    exchanged = []
    for i, j in enumerate(order):
        cols = pl.ds(pl.multiple_of(j * 1536, 1536), 1536)
        exchanged.append(copies.send(act.at[:, :, cols], a_v.at[i, 1], dev(c_=1 - c)))

    def first(t, sub, pool):
        axis = STAGES[t][0]
        if t == 0:
            view, pos = pan.at[0, :, 2 * sub:2 * sub + 2], 0
        else:
            view, pos = pan.at[t, pl.ds(2 * order[sub], 2)], t

        def piece(dest):
            return view[(slice(None),) * pos + (dest,)]

        def to(dest):
            return dev(**{axis + "_": dest})

        total = yield from ring(copies, SIZE[axis], me[axis], piece, 1, to, *pool[:8])
        if t == 0:
            mid[0][2 * sub:2 * sub + 2] = total
            return
        j = order[sub]
        mid[t][pl.ds(2 * j, 2)] = total
        second = STAGES[t][1]
        ready[t][pl.ds(2 * j, 2)] = yield from direct(
            copies, SIZE[second], me[second], lambda dest: mid[t][pl.ds(2 * j, 2), dest],
            lambda dest: dev(**{second + "_": dest}), *pool[8:])
        for dest in (2 * j, 2 * j + 1) if sub < 3 else (2 * j + 1 - zz,):
            d = lax.rem(dest - z + NZ, NZ)
            copies.make(ready[t].at[dest], got[t].at[d - 1], dev(z_=dest), base[t] + d - 1).start()

    def rest(t, pool):
        if t == 0:
            total = yield from direct(copies, NY, y, lambda d: mid[0][d], lambda d: dev(y_=d), *pool[0:2])
            pool[2][...] = total
            total = yield from direct(copies, NX, x, lambda d: pool[2][d], lambda d: dev(x_=d), *pool[3:5])
        else:
            total = ready[t][z]
            for d in range(1, NZ):
                to = lax.rem(z + d, NZ)
                copy = copies.make(ready[t].at[to], got[t].at[d - 1], dev(z_=to), base[t] + d - 1)
                copy.wait_recv()
                copies.made.append(copy)
                total = total + got[t][d - 1]
        p_v[c, x, 16 * t:16 * t + 16, :] = total * (1.0 / 65536.0)

    mid = [bufs.pop(0) for _ in range(3)]
    ready = [None] + [bufs.pop(0) for _ in range(2)]
    got = [None] + [bufs.pop(0) for _ in range(2)]
    base = [None] + [copies.take(NZ - 1) for _ in range(2)]
    rings = []
    for t in range(3):
        subs = []
        for sub in range(2 if t == 0 else 4):
            size = 8 if t == 0 else 10
            subs.append(first(t, sub, bufs[:size]))
            bufs = bufs[size:]
        rings.append(subs)
    rests = [rest(0, bufs), rest(1, ()), rest(2, ())]

    def run(*names):
        for name in names:
            t, sub = name // 10, name % 10
            next(rests[t] if sub == 9 else rings[t][sub], None)

    def compute(i):
        j = order[i]
        b_loads[i].wait()
        own_loads[i].wait()
        proj[0:256, :] = jnp.dot(a_v[i, 0].reshape(256, 1536), b_v[i], preferred_element_type=F32).astype(BF16)
        exchanged[i].wait_recv()
        proj[256:512, :] = jnp.dot(a_v[i, 1].reshape(256, 1536), b_v[i], preferred_element_type=F32).astype(BF16)
        for k in range(4):
            lhs = a_v[i, :, :, :, 384 * k:384 * k + 384].reshape(512, 384)
            r = lax.dot_general(lhs, proj[...], (((0,), (0,)), ((), ())), preferred_element_type=F32)
            r = r.reshape(2, 4, 3, 16, 256)
            for t in range(3):
                pan[t, 2 * j + k // 2, 2 * (k % 2):2 * (k % 2) + 2] = r[:, :, t]

    compute(0)
    run(0, 1, 10, 20)
    compute(1)
    run(11, 21)
    compute(2)
    run(12, 22, 0, 1, 10, 20)
    compute(3)
    run(13, 23, 11, 21, 0, 1, 12, 22, 10, 20, 13, 23, 11, 21, 0, 1, 12, 22)
    run(10, 20, 13, 23, 11, 21, 0, 1, 9, 12, 22, 13, 23, 9, 19, 29, 9)

    sent = []
    for d in range(1, NX):
        sent.append(copies.send(p_v.at[c, x], p_v.at[c, x], dev(x_=lax.rem(x + d, NX))))
    swap = copies.send(p_v.at[c, x], p_v.at[c, x], dev(c_=1 - c))
    passed = [swap]
    for d in range(1, NX):
        sent[d - 1].wait_recv()
        other = lax.rem(x + NX - d, NX)
        passed.append(copies.send(p_v.at[c, other], p_v.at[c, other], dev(c_=1 - c)))
    for copy in passed:
        copy.wait_recv()

    for h in range(2):
        rows_v[:, 256 * h:256 * h + 256] = p_v[h].reshape(192, 256)
    def gram(b):
        lo = 128 * b
        gs[b, :, :, :, lo:] = lax.dot_general(
            rows_v[:, lo:lo + 128], rows_v[:, lo:], (((0,), (0,)), ((), ())), precision=HI,
            preferred_element_type=F32).reshape(8, 2, 8, 512 - lo)

    q_me = c * NX + x
    p_me = zz * NY + y
    parts = (pl.ds(0, 1), pl.ds(1, NB - 1))

    def peer(d):
        q = lax.rem(p_me + d, 8)
        return q, dev(z_=z - zz + q // NY, y_=lax.rem(q, NY))

    def cols(p):
        return pl.ds(pl.multiple_of(lax.rem(p, NB) * 128, 128), 128)

    reduced = [[], []]
    for h, part in enumerate(parts):
        for b in range(1) if h == 0 else range(1, NB):
            gram(b)
        for d in range(1, 8):
            p, to = peer(d)
            reduced[h].append(copies.send(
                gs.at[part, q_me, p // NB, :, cols(p)], gr.at[d - 1, part], to))
    spread = [[], []]
    for h, part in enumerate(parts):
        total = gs[part, q_me, p_me // NB, :, cols(p_me)]
        for d in range(1, 8):
            reduced[h][d - 1].wait_recv()
            total = total + gr[d - 1, part]
        g_v[part, c, x, p_me // NB, lax.rem(p_me, NB)] = total
        for d in range(1, 8):
            mine = g_v.at[part, c, x, p_me // NB, lax.rem(p_me, NB)]
            spread[h].append(copies.send(mine, mine, peer(d)[1]))
    diagonal, across, swapped = [], [[] for _ in range(NB)], []

    def spread_x(b):
        for d in range(1, NX):
            mine = g_v.at[b, c, x, :, max(b, 1):]
            across[b].append(copies.send(mine, mine, dev(x_=lax.rem(x + d, NX))))

    for copy in spread[0]:
        copy.wait_recv()
    for d in range(1, 8):
        mine = g_v.at[0, c, x, :, 0]
        diagonal.append(copies.send(
            mine, mine, dev(x_=lax.rem(x + d // 2, NX), c_=c if d % 2 == 0 else 1 - c)))
    spread_x(0)
    for copy in spread[1]:
        copy.wait_recv()
    for b in range(1, NB):
        spread_x(b)

    def swap_cores(b):
        for copy in across[b]:
            copy.wait_recv()
        mine = g_v.at[b, c, :, :, max(b, 1):]
        swapped.append(copies.send(mine, mine, dev(c_=1 - c)))

    def take(b, first, last):
        for q in range(8):
            for rt in range(2):
                for ct in range(first, last):
                    up[b, 16 * q + 8 * rt:16 * q + 8 * rt + 8, 128 * ct:128 * ct + 128] = (
                        g_v[b, q // NX, q % NX, rt, ct])

    def arrive(b):
        swapped[b].wait_recv()
        take(b, max(b, 1), NB)

    for copy in diagonal:
        copy.wait_recv()
    take(0, 0, 1)
    for b in range(NB):
        lo, hi = 128 * b, 128 * b + 128

        def between(strip):
            if b == 0 and strip in (3, 5, 8, 9):
                swap_cores((3, 5, 8, 9).index(strip))

        inv = jnp.concatenate(
            diag_inverse([up[b, 8 * i:8 * i + 8, lo:hi] for i in range(16)], between), axis=0)
        if b == 0:
            for e in range(NB):
                arrive(e)
        if b < NB - 1:
            u = jnp.dot(inv, up[b, :, hi:], precision=HI, preferred_element_type=F32)
            for e in range(b + 1, NB):
                off = 128 * (e - b - 1)
                up[e, :, 128 * e:] -= lax.dot_general(
                    u[:, off:off + 128], u[:, off:], (((0,), (0,)), ((), ())), precision=HI,
                    preferred_element_type=F32)
        solved = lax.dot_general(rows_v[:, lo:hi], inv, (((1,), (1,)), ((), ())), precision=HI,
                                 preferred_element_type=F32)
        out_v[:, lo:hi] = solved * math.sqrt(1536.0)
        if b < NB - 1:
            rows_v[:, hi:] -= jnp.dot(solved, u, precision=HI, preferred_element_type=F32)
    written = pltpu.make_async_copy(out_v, out, out_sems.at[0])
    written.start()
    for copy in copies.made:
        copy.wait_send()
    written.wait()


def refreshed(act, basis):
    tile = (16, 256)
    bufs = [pltpu.VMEM((NY, NX) + tile, F32), pltpu.VMEM((NZ, NX) + tile, F32), pltpu.VMEM((NZ, NY) + tile, F32)]
    bufs += [pltpu.VMEM((NZ,) + tile, F32)] * 2 + [pltpu.VMEM((NZ - 1,) + tile, F32)] * 2
    for t, axes in enumerate(STAGES):
        steps = SIZE[axes[0]] // 2
        full = (2, 4) + tile
        for _ in range(2 if t == 0 else 4):
            bufs += [pltpu.VMEM((steps - 1,) + full, BF16)] * 4 + [pltpu.VMEM((1,) + full[1:], BF16)] * 4
            if t:
                bufs += [pltpu.VMEM((3, 2) + tile, BF16)] * 2
    bufs += [pltpu.VMEM((NY - 1, NX) + tile, BF16)] * 2 + [pltpu.VMEM((NX,) + tile, F32)]
    bufs += [pltpu.VMEM((NX - 1,) + tile, F32)] * 2
    return pl.pallas_call(
        kernel,
        out_shape=jax.ShapeDtypeStruct((192, 512), F32),
        in_specs=[pl.BlockSpec(memory_space=pl.ANY)] * 2,
        out_specs=pl.BlockSpec(memory_space=pl.ANY),
        scratch_shapes=[
            pltpu.VMEM((4, 2, 4, 64, 1536), BF16),
            pltpu.VMEM((4, 1536, 256), BF16),
            pltpu.VMEM((512, 256), BF16),
            pltpu.VMEM((3, NZ, NY, NX, 16, 256), F32),
            pltpu.VMEM((NC, NX, 48, 256), F32),
            pltpu.VMEM((NB, NC, NX, 2, NB, 8, 128), F32),
            pltpu.VMEM((NB, 8, 2, 8, 512), F32),
            pltpu.VMEM((7, NB, 8, 128), F32),
            pltpu.VMEM((NB, 128, 512), F32),
            pltpu.VMEM((192, 512), F32),
            pltpu.VMEM((192, 512), F32),
            pltpu.SemaphoreType.DMA((8,)),
            pltpu.SemaphoreType.DMA((192,)),
            pltpu.SemaphoreType.DMA((192,)),
            pltpu.SemaphoreType.DMA((1,)),
        ] + bufs,
        compiler_params=pltpu.CompilerParams(
            collective_id=1, has_side_effects=True, vmem_limit_bytes=56 * 2**20),
    )(act, basis)


def on_device(activations, prev_basis):
    return refreshed(activations, prev_basis)


def solution(mesh):
    in_specs = (P(None, ("dp", "seq"), None), P())
    out_specs = P("seq", None)
    return jax.shard_map(
        on_device, mesh=mesh, in_specs=in_specs, out_specs=out_specs, check_vma=False
    )
```

```python
import functools
import math

import jax
import jax.numpy as jnp
from jax import lax
from jax.experimental import pallas as pl
from jax.experimental.pallas import tpu as pltpu
from jax.sharding import PartitionSpec as P

F32, BF16 = jnp.float32, jnp.bfloat16
NX, NC, NZ, NY, NB = 4, 2, 8, 4, 4
HI = lax.Precision.HIGHEST
STAGES = (("z", "y", "x"), ("y", "x", "z"), ("x", "y", "z"))
SIZE = {"x": NX, "y": NY, "z": NZ}


def splat_lane(v, k):
    return jnp.broadcast_to(v[:, k:k + 1], (8, 128))


def splat_row(v, k):
    return jnp.broadcast_to(v[k:k + 1, :], (8, 128))


def three_terms(v):
    high = v.astype(BF16).astype(F32)
    left = v - high
    middle = left.astype(BF16).astype(F32)
    return high, middle, left - middle


def diag_inverse(a, between):
    n = len(a)
    sub = lax.broadcasted_iota(jnp.int32, (8, 128), 0)
    lane = lax.broadcasted_iota(jnp.int32, (8, 128), 1)
    out = []
    col = [splat_lane(a[0], j) for j in range(8)]
    for s in range(n):
        c0 = 8 * s
        r = a[s]
        ahead = s + 1 < n
        if ahead:
            ncol = [splat_lane(a[s + 1], c0 + j) for j in range(8)]
        inv_rows = jnp.zeros((8, 128), F32)
        factors = []
        for k in range(8):
            inv = 1.0 / splat_row(col[k], k)
            inv_rows = jnp.where(sub == k, inv, inv_rows)
            m = jnp.where(sub > k, col[k] * inv, 0.0)
            if ahead:
                factors.append(ncol[k] * inv)
            if k < 7:
                row = jnp.where(lane == c0 + k, 1.0, splat_row(r, k))
                r = jnp.where((lane == c0 + k) & (sub > k), 0.0, r) - m * row
                for j in range(k + 1, 8):
                    top = splat_row(col[j], k)
                    col[j] = col[j] - m * top
                    if ahead:
                        ncol[j] = ncol[j] - factors[k] * top
        rel = lane - c0 - sub
        rp = jnp.where(rel == 0, 1.0, jnp.where((rel > 0) & (lane < c0 + 8), 0.0, r))
        out.append(jnp.where(lane < c0 + 8, rp, 0.0) * jnp.sqrt(inv_rows))
        strip = (lane >= c0) & (lane < c0 + 8)
        if ahead:
            acc = jnp.where(strip, 0.0, a[s + 1])
            for k in range(8):
                acc = acc - factors[k] * splat_row(rp, k)
            a[s + 1] = acc
            col = [splat_lane(acc, c0 + 8 + j) for j in range(8)]
        if s + 2 < n:
            uh, um, ul = three_terms(r * inv_rows)
            rh, rm, rl = three_terms(rp)
            left = jnp.concatenate([uh, uh, um, uh, ul, um], axis=0).astype(BF16)
            right = jnp.concatenate([rh, rm, rh, rl, rh, rm], axis=0).astype(BF16)
            update = lax.dot_general(left, right, (((0,), (0,)), ((), ())), preferred_element_type=F32)
            for t in range(s + 2, n):
                a[t] = jnp.where(strip, 0.0, a[t]) - update[8 * t:8 * t + 8, :]
        between(s)
    return out


class Copies:
    def __init__(self, send_sems, recv_sems):
        self.send_sems, self.recv_sems, self.count, self.made = send_sems, recv_sems, 0, []

    def take(self, number):
        self.count += number
        return self.count - number

    def make(self, src, dst, device, n):
        return pltpu.make_async_remote_copy(
            src_ref=src, dst_ref=dst, send_sem=self.send_sems.at[n], recv_sem=self.recv_sems.at[n],
            device_id=device, device_id_type=pl.DeviceIdType.MESH,
        )

    def send(self, src, dst, device):
        copy = self.make(src, dst, device, self.take(1))
        copy.start()
        self.made.append(copy)
        return copy


def ring(copies, n, me, piece, half, to, up_s, up_r, dn_s, dn_r, up_h, dn_h, up_hr, dn_hr):
    steps = n // 2
    far = piece(lax.rem(me + steps, n))
    up_h[...] = far[:half].astype(BF16)
    dn_h[...] = far[half:].astype(BF16)
    up = copies.send(up_h, up_hr, to(lax.rem(me + 1, n)))
    dn = copies.send(dn_h, dn_hr, to(lax.rem(me + n - 1, n)))
    yield
    for i in range(1, steps):
        d = steps - i
        mine = piece(lax.rem(me + d, n))
        up.wait_recv()
        if i == 1:
            up_s[0, :half] = (mine[:half] + up_hr[...].astype(F32)).astype(BF16)
            up_s[0, half:] = mine[half:].astype(BF16)
        else:
            up_s[i - 1] = (mine + up_r[i - 2].astype(F32)).astype(BF16)
        up = copies.send(up_s.at[i - 1], up_r.at[i - 1], to(lax.rem(me + 1, n)))
        mine = piece(lax.rem(me + n - d, n))
        dn.wait_recv()
        if i == 1:
            dn_s[0, half:] = (mine[half:] + dn_hr[...].astype(F32)).astype(BF16)
            dn_s[0, :half] = mine[:half].astype(BF16)
        else:
            dn_s[i - 1] = (mine + dn_r[i - 2].astype(F32)).astype(BF16)
        dn = copies.send(dn_s.at[i - 1], dn_r.at[i - 1], to(lax.rem(me + n - 1, n)))
        yield
    up.wait_recv()
    dn.wait_recv()
    return piece(me) + up_r[steps - 2].astype(F32) + dn_r[steps - 2].astype(F32)


def direct(copies, n, me, piece, to, bufs, bufr):
    sent = []
    for d in range(1, n):
        bufs[d - 1] = piece(lax.rem(me + d, n)).astype(bufs.dtype)
        sent.append(copies.send(bufs.at[d - 1], bufr.at[d - 1], to(lax.rem(me + d, n))))
    yield
    total = piece(me)
    for d in range(1, n):
        sent[d - 1].wait_recv()
        total = total + bufr[d - 1].astype(F32)
    return total


def kernel(act, basis, out, *scratch):
    (a_v, b_v, proj, pan, p_v, g_v, gs, gr, up, rows_v, out_v, load_sems, send_sems, recv_sems, out_sems,
     *bufs) = scratch
    bufs = list(bufs)
    dp, seq = lax.axis_index("dp"), lax.axis_index("seq")
    x, c, z, y = dp // 2, lax.rem(dp, 2), seq // NY, lax.rem(seq, NY)
    zz = lax.rem(z, 2)
    me = {"x": x, "y": y, "z": z}

    def dev(x_=None, c_=None, z_=None, y_=None):
        x_, c_, z_, y_ = (x if x_ is None else x_, c if c_ is None else c_,
                          z if z_ is None else z_, y if y_ is None else y_)
        return (x_ * NC + c_, z_ * NY + y_)

    peers = [dev(c_=1 - c)]
    for d in range(1, NX):
        peers.append(dev(x_=lax.rem(x + d, NX)))
    for d in range(1, NY):
        peers += [dev(y_=lax.rem(y + d, NY)), dev(z_=z + 1 - 2 * zz, y_=lax.rem(y + d, NY))]
    for d in range(1, NZ):
        peers.append(dev(z_=lax.rem(z + d, NZ)))
    barrier = pltpu.get_barrier_semaphore()
    for peer in peers:
        pl.semaphore_signal(barrier, inc=1, device_id=peer, device_id_type=pl.DeviceIdType.MESH)

    order = [lax.rem(z // 2 + o, 4) for o in (2, 1, 3, 0)]
    own_loads, b_loads = [], []
    for i, j in enumerate(order):
        cols = pl.ds(pl.multiple_of(j * 1536, 1536), 1536)
        b_loads.append(pltpu.make_async_copy(
            basis.at[j, :, pl.ds(pl.multiple_of(c * 256, 256), 256)], b_v.at[i], load_sems.at[i]))
        own_loads.append(pltpu.make_async_copy(act.at[:, :, cols], a_v.at[i, 0], load_sems.at[4 + i]))
        own_loads[i].start()
        b_loads[i].start()

    pl.semaphore_wait(barrier, len(peers))

    copies = Copies(send_sems, recv_sems)
    exchanged = []
    for i, j in enumerate(order):
        cols = pl.ds(pl.multiple_of(j * 1536, 1536), 1536)
        exchanged.append(copies.send(act.at[:, :, cols], a_v.at[i, 1], dev(c_=1 - c)))

    def first(t, sub, pool):
        axis = STAGES[t][0]
        if t == 0:
            view, pos = pan.at[0, :, 2 * sub:2 * sub + 2], 0
        else:
            view, pos = pan.at[t, pl.ds(2 * order[sub], 2)], t

        def piece(dest):
            return view[(slice(None),) * pos + (dest,)]

        def to(dest):
            return dev(**{axis + "_": dest})

        total = yield from ring(copies, SIZE[axis], me[axis], piece, 1, to, *pool[:8])
        if t == 0:
            mid[0][2 * sub:2 * sub + 2] = total
            return
        j = order[sub]
        mid[t][pl.ds(2 * j, 2)] = total
        second = STAGES[t][1]
        ready[t][pl.ds(2 * j, 2)] = yield from direct(
            copies, SIZE[second], me[second], lambda dest: mid[t][pl.ds(2 * j, 2), dest],
            lambda dest: dev(**{second + "_": dest}), *pool[8:])
        for dest in (2 * j, 2 * j + 1) if sub < 3 else (2 * j + 1 - zz,):
            d = lax.rem(dest - z + NZ, NZ)
            copies.make(ready[t].at[dest], got[t].at[d - 1], dev(z_=dest), base[t] + d - 1).start()

    def rest(t, pool):
        if t == 0:
            total = yield from direct(copies, NY, y, lambda d: mid[0][d], lambda d: dev(y_=d), *pool[0:2])
            pool[2][...] = total
            total = yield from direct(copies, NX, x, lambda d: pool[2][d], lambda d: dev(x_=d), *pool[3:5])
        else:
            total = ready[t][z]
            for d in range(1, NZ):
                to = lax.rem(z + d, NZ)
                copy = copies.make(ready[t].at[to], got[t].at[d - 1], dev(z_=to), base[t] + d - 1)
                copy.wait_recv()
                copies.made.append(copy)
                total = total + got[t][d - 1]
        p_v[c, x, 16 * t:16 * t + 16, :] = total * (1.0 / 65536.0)

    mid = [bufs.pop(0) for _ in range(3)]
    ready = [None] + [bufs.pop(0) for _ in range(2)]
    got = [None] + [bufs.pop(0) for _ in range(2)]
    base = [None] + [copies.take(NZ - 1) for _ in range(2)]
    rings = []
    for t in range(3):
        subs = []
        for sub in range(2 if t == 0 else 4):
            size = 8 if t == 0 else 10
            subs.append(first(t, sub, bufs[:size]))
            bufs = bufs[size:]
        rings.append(subs)
    rests = [rest(0, bufs), rest(1, ()), rest(2, ())]

    def run(*names):
        for name in names:
            t, sub = name // 10, name % 10
            next(rests[t] if sub == 9 else rings[t][sub], None)

    def compute(i):
        j = order[i]
        b_loads[i].wait()
        own_loads[i].wait()
        proj[0:256, :] = jnp.dot(a_v[i, 0].reshape(256, 1536), b_v[i], preferred_element_type=F32).astype(BF16)
        exchanged[i].wait_recv()
        proj[256:512, :] = jnp.dot(a_v[i, 1].reshape(256, 1536), b_v[i], preferred_element_type=F32).astype(BF16)
        for k in range(4):
            lhs = a_v[i, :, :, :, 384 * k:384 * k + 384].reshape(512, 384)
            r = lax.dot_general(lhs, proj[...], (((0,), (0,)), ((), ())), preferred_element_type=F32)
            r = r.reshape(2, 4, 3, 16, 256)
            for t in range(3):
                pan[t, 2 * j + k // 2, 2 * (k % 2):2 * (k % 2) + 2] = r[:, :, t]

    compute(0)
    run(0, 1, 10, 20)
    compute(1)
    run(11, 21)
    compute(2)
    run(12, 22, 0, 1, 10, 20)
    compute(3)
    run(13, 23, 11, 21, 0, 1, 12, 22, 10, 20, 13, 23, 11, 21, 0, 1, 12, 22)
    run(10, 20, 13, 23, 11, 21, 0, 1, 9, 12, 22, 13, 23, 9, 19, 29, 9)

    sent = []
    for d in range(1, NX):
        sent.append(copies.send(p_v.at[c, x], p_v.at[c, x], dev(x_=lax.rem(x + d, NX))))
    swap = copies.send(p_v.at[c, x], p_v.at[c, x], dev(c_=1 - c))
    passed = [swap]
    for d in range(1, NX):
        sent[d - 1].wait_recv()
        other = lax.rem(x + NX - d, NX)
        passed.append(copies.send(p_v.at[c, other], p_v.at[c, other], dev(c_=1 - c)))
    for copy in passed:
        copy.wait_recv()

    for h in range(2):
        rows_v[:, 256 * h:256 * h + 256] = p_v[h].reshape(192, 256)
    def gram(b):
        lo = 128 * b
        gs[b, :, :, :, lo:] = lax.dot_general(
            rows_v[:, lo:lo + 128], rows_v[:, lo:], (((0,), (0,)), ((), ())), precision=HI,
            preferred_element_type=F32).reshape(8, 2, 8, 512 - lo)

    q_me = c * NX + x
    p_me = zz * NY + y
    parts = (pl.ds(0, 1), pl.ds(1, NB - 1))

    def peer(d):
        q = lax.rem(p_me + d, 8)
        return q, dev(z_=z - zz + q // NY, y_=lax.rem(q, NY))

    def cols(p):
        return pl.ds(pl.multiple_of(lax.rem(p, NB) * 128, 128), 128)

    reduced = [[], []]
    for h, part in enumerate(parts):
        for b in range(1) if h == 0 else range(1, NB):
            gram(b)
        for d in range(1, 8):
            p, to = peer(d)
            reduced[h].append(copies.send(
                gs.at[part, q_me, p // NB, :, cols(p)], gr.at[d - 1, part], to))
    spread = [[], []]
    for h, part in enumerate(parts):
        total = gs[part, q_me, p_me // NB, :, cols(p_me)]
        for d in range(1, 8):
            reduced[h][d - 1].wait_recv()
            total = total + gr[d - 1, part]
        g_v[part, c, x, p_me // NB, lax.rem(p_me, NB)] = total
        for d in range(1, 8):
            mine = g_v.at[part, c, x, p_me // NB, lax.rem(p_me, NB)]
            spread[h].append(copies.send(mine, mine, peer(d)[1]))
    diagonal, across, swapped = [], [[] for _ in range(NB)], []

    def spread_x(b):
        for d in range(1, NX):
            mine = g_v.at[b, c, x, :, max(b, 1):]
            across[b].append(copies.send(mine, mine, dev(x_=lax.rem(x + d, NX))))

    for copy in spread[0]:
        copy.wait_recv()
    for d in range(1, 8):
        mine = g_v.at[0, c, x, :, 0]
        diagonal.append(copies.send(
            mine, mine, dev(x_=lax.rem(x + d // 2, NX), c_=c if d % 2 == 0 else 1 - c)))
    spread_x(0)
    for copy in spread[1]:
        copy.wait_recv()
    for b in range(1, NB):
        spread_x(b)

    def swap_cores(b):
        for copy in across[b]:
            copy.wait_recv()
        mine = g_v.at[b, c, :, :, max(b, 1):]
        swapped.append(copies.send(mine, mine, dev(c_=1 - c)))

    def take(b, first, last):
        for q in range(8):
            for rt in range(2):
                for ct in range(first, last):
                    up[b, 16 * q + 8 * rt:16 * q + 8 * rt + 8, 128 * ct:128 * ct + 128] = (
                        g_v[b, q // NX, q % NX, rt, ct])

    def arrive(b):
        swapped[b].wait_recv()
        take(b, max(b, 1), NB)

    for copy in diagonal:
        copy.wait_recv()
    take(0, 0, 1)
    for b in range(NB):
        lo, hi = 128 * b, 128 * b + 128

        def between(strip):
            if b == 0 and strip in (1, 2, 3, 4):
                swap_cores((1, 2, 3, 4).index(strip))

        inv = jnp.concatenate(
            diag_inverse([up[b, 8 * i:8 * i + 8, lo:hi] for i in range(16)], between), axis=0)
        if b == 0:
            for e in range(NB):
                arrive(e)
        if b < NB - 1:
            u = jnp.dot(inv, up[b, :, hi:], precision=HI, preferred_element_type=F32)
            for e in range(b + 1, NB):
                off = 128 * (e - b - 1)
                up[e, :, 128 * e:] -= lax.dot_general(
                    u[:, off:off + 128], u[:, off:], (((0,), (0,)), ((), ())), precision=HI,
                    preferred_element_type=F32)
        solved = lax.dot_general(rows_v[:, lo:hi], inv, (((1,), (1,)), ((), ())), precision=HI,
                                 preferred_element_type=F32)
        out_v[:, lo:hi] = solved * math.sqrt(1536.0)
        if b < NB - 1:
            rows_v[:, hi:] -= jnp.dot(solved, u, precision=HI, preferred_element_type=F32)
    written = pltpu.make_async_copy(out_v, out, out_sems.at[0])
    written.start()
    for copy in copies.made:
        copy.wait_send()
    written.wait()


def refreshed(act, basis):
    tile = (16, 256)
    bufs = [pltpu.VMEM((NY, NX) + tile, F32), pltpu.VMEM((NZ, NX) + tile, F32), pltpu.VMEM((NZ, NY) + tile, F32)]
    bufs += [pltpu.VMEM((NZ,) + tile, F32)] * 2 + [pltpu.VMEM((NZ - 1,) + tile, F32)] * 2
    for t, axes in enumerate(STAGES):
        steps = SIZE[axes[0]] // 2
        full = (2, 4) + tile
        for _ in range(2 if t == 0 else 4):
            bufs += [pltpu.VMEM((steps - 1,) + full, BF16)] * 4 + [pltpu.VMEM((1,) + full[1:], BF16)] * 4
            if t:
                bufs += [pltpu.VMEM((3, 2) + tile, BF16)] * 2
    bufs += [pltpu.VMEM((NY - 1, NX) + tile, BF16)] * 2 + [pltpu.VMEM((NX,) + tile, F32)]
    bufs += [pltpu.VMEM((NX - 1,) + tile, F32)] * 2
    return pl.pallas_call(
        kernel,
        out_shape=jax.ShapeDtypeStruct((192, 512), F32),
        in_specs=[pl.BlockSpec(memory_space=pl.ANY)] * 2,
        out_specs=pl.BlockSpec(memory_space=pl.ANY),
        scratch_shapes=[
            pltpu.VMEM((4, 2, 4, 64, 1536), BF16),
            pltpu.VMEM((4, 1536, 256), BF16),
            pltpu.VMEM((512, 256), BF16),
            pltpu.VMEM((3, NZ, NY, NX, 16, 256), F32),
            pltpu.VMEM((NC, NX, 48, 256), F32),
            pltpu.VMEM((NB, NC, NX, 2, NB, 8, 128), F32),
            pltpu.VMEM((NB, 8, 2, 8, 512), F32),
            pltpu.VMEM((7, NB, 8, 128), F32),
            pltpu.VMEM((NB, 128, 512), F32),
            pltpu.VMEM((192, 512), F32),
            pltpu.VMEM((192, 512), F32),
            pltpu.SemaphoreType.DMA((8,)),
            pltpu.SemaphoreType.DMA((192,)),
            pltpu.SemaphoreType.DMA((192,)),
            pltpu.SemaphoreType.DMA((1,)),
        ] + bufs,
        compiler_params=pltpu.CompilerParams(
            collective_id=1, has_side_effects=True, vmem_limit_bytes=56 * 2**20),
    )(act, basis)


def on_device(activations, prev_basis):
    return refreshed(activations, prev_basis)


def solution(mesh):
    in_specs = (P(None, ("dp", "seq"), None), P())
    out_specs = P("seq", None)
    return jax.shard_map(
        on_device, mesh=mesh, in_specs=in_specs, out_specs=out_specs, check_vma=False
    )
```
